32 devices in a mesh: gx: 4 (over x, core), gy: 2 (over y), gz: 4 (over z).
Axes of the slice: x: 2, y: 2, z: 4, core: 2. Of those that a mesh axis runs over, the one named last changes fastest.
Arguments:
- right_side: float32 [32, 16, 512], P('gx', 'gy', 'gz'), may hold values from -8 to 8
- geometry: float32 [4, 32, 16, 512], P(None, 'gx', 'gy', 'gz'), may hold values from 0.02 to 0.2
- element_shape_class: int32 [4, 2, 64], P('gx', 'gy', 'gz'), may hold values from 0 to 31
- fdm_vectors: float32 [32, 3, 10, 10], replicated, may hold values from -1 to 2
- fdm_values: float32 [32, 3, 10], replicated, may hold values from 0.3 to 10
Outputs:
- solution: float32 [32, 16, 512], P('gx', 'gy', 'gz')
- residual: float32 [32, 16, 512], P('gx', 'gy', 'gz')
The draws below stay inside these ranges and needn't reach their ends.
All inputs are finite; a program needn't handle non-finite values.
Results may differ from the reference program's by a relative error of at most 0.0003.
Values sent between devices are 32-bit elements; how exact they have to be, the bound alone decides.
A program may use at most 64 MiB of HBM per device.

```python
import math
import jax
import jax.numpy as jnp
import numpy as np
from jax import lax

EXTENDED = 10
SHAPE_CLASSES = 32
ITERS = 2
ELEMENTS_FIRST = 4
ELEMENTS_SECOND = 2
ELEMENTS_THIRD = 64
NX = 32
NY = 16
NZ = 512


def unique_index(length):
    position = jnp.arange(length, dtype=jnp.int32)
    return position // 8 * 7 + position % 8


def draw_right_side(key, part):
    count_x = 7 * ELEMENTS_FIRST + 1
    count_y = 7 * ELEMENTS_SECOND + 1
    count_along_depth = 7 * ELEMENTS_THIRD + 1
    along_first = jnp.arange(count_x, dtype=jnp.float32) / count_x
    along_second = jnp.arange(count_y, dtype=jnp.float32) / count_y
    along_third = jnp.arange(count_along_depth, dtype=jnp.float32) / count_along_depth
    scale_field = jnp.sqrt(1.0 + 2.0 * (along_first[:, None, None] + along_second[None, :, None] + along_third[None, None, :]) / 3.0)
    base_values = jax.random.truncated_normal(key, -4.0, 4.0, (count_x, count_y, count_along_depth), jnp.float32)
    unique_field = base_values * scale_field
    spread = jnp.take(unique_field, unique_index(NX), axis=0)
    spread = jnp.take(spread, unique_index(NY), axis=1)
    return jnp.take(spread, unique_index(NZ), axis=2)


def draw_fdm_vectors(key, part):
    full_shape = (SHAPE_CLASSES, 3, EXTENDED, EXTENDED)
    identity = (lax.broadcasted_iota(jnp.int32, full_shape, 2) == lax.broadcasted_iota(jnp.int32, full_shape, 3)).astype(jnp.float32)
    spread = 0.25 * jax.random.truncated_normal(key, -3.0, 3.0, full_shape, jnp.float32)
    return identity + spread


def touch_ends(drawn, rng, least, high):
    spot = [jax.random.randint(jax.random.fold_in(rng, axis), (), 0, length) for axis, length in enumerate(drawn.shape)]
    longest = drawn.shape.index(max(drawn.shape))
    neighbour = spot[:longest] + [(spot[longest] + 1) % drawn.shape[longest]] + spot[longest + 1:]
    return drawn.at[tuple(spot)].set(least).at[tuple(neighbour)].set(high)


def levels(key, dims, cuts, low, largest):
    def one(axis_at, blocks):
        steps = jax.random.uniform(jax.random.fold_in(jax.random.fold_in(key, 6), axis_at), (blocks,), jnp.float32, low / len(cuts), largest / len(cuts))
        return jnp.repeat(jnp.exp(steps), dims[axis_at] // blocks).reshape((-1,) + (1,) * (len(dims) - axis_at - 1))

    level = one(*cuts[0])
    for cut in cuts[1:]:
        level = level * one(*cut)
    return level


def setup_inputs(seed: int = 0) -> dict:
    keys = jax.random.split(jax.random.key(seed), 6)
    right_side = draw_right_side(jax.random.fold_in(keys[5], 71), 0)
    geometry = jnp.clip(jnp.exp(math.log(0.2) - 2.3025851 * jax.random.uniform(keys[1], (4, NX, NY, NZ), jnp.float32) ** levels(keys[1], (4, NX, NY, NZ), ((1, 4), (2, 2), (3, 4)), -0.2, 0.2)), 0.02, 0.2)
    element_shape_class = touch_ends(jax.random.randint(keys[2], (ELEMENTS_FIRST, ELEMENTS_SECOND, ELEMENTS_THIRD), 0, SHAPE_CLASSES), jax.random.fold_in(keys[2], 1), 0, SHAPE_CLASSES - 1).astype(jnp.int32)
    fdm_vectors = draw_fdm_vectors(jax.random.fold_in(keys[5], 71), 0)
    fdm_values = jnp.clip(jnp.exp(jax.random.uniform(keys[4], (SHAPE_CLASSES, 3, EXTENDED), jnp.float32, math.log(0.3), math.log(10.0))), 0.3, 10.0)
    return {"right_side": right_side, "geometry": geometry, "element_shape_class": element_shape_class, "fdm_vectors": fdm_vectors, "fdm_values": fdm_values}


HIGHEST = lax.Precision.HIGHEST
FORWARD_FORMS = ("ai,eiyz->eayz", "aj,xejz->xeaz", "ak,xyek->xyea")


def derivative_table():
    points = np.array([-1.0, -0.8717401485096066, -0.5917001814331423, -0.2092992179024789,
                       0.2092992179024789, 0.5917001814331423, 0.8717401485096066, 1.0])
    previous = np.ones(8)
    current = points * 1.0
    for order in range(1, 7):
        following = ((2 * order + 1) * points * current - order * previous) / (order + 1)
        previous = current
        current = following
    legendre = current
    spacing = points[:, None] - points[None, :] + np.eye(8)
    off_diagonal = legendre[:, None] / (legendre[None, :] * spacing)
    positions = np.arange(8)
    end_values = np.where(positions == 0, -14.0, 0.0) + np.where(positions == 7, 14.0, 0.0)
    return np.where(np.eye(8) > 0, np.eye(8) * end_values[None, :], off_diagonal)


def apply_along(field, matrix, dim_index):
    sizes = list(field.shape)
    split_shape = sizes[:dim_index] + [sizes[dim_index] // 8, 8] + sizes[dim_index + 1:]
    blocks = field.reshape(split_shape)
    return jnp.einsum(FORWARD_FORMS[dim_index], matrix, blocks, precision=HIGHEST).reshape(sizes)


def local_operator(field, geometry, derivative):
    total = geometry[3] * field
    for dim_index in range(3):
        gradient = apply_along(field, derivative, dim_index)
        total = total + apply_along(geometry[dim_index] * gradient, derivative.T, dim_index)
    return total


def pair_add(padded, dim_index):
    length = padded.shape[dim_index] - 2
    middle = lax.slice_in_dim(padded, 1, length + 1, axis=dim_index)
    following = lax.slice_in_dim(padded, 2, length + 2, axis=dim_index)
    previous = lax.slice_in_dim(padded, 0, length, axis=dim_index)
    position = lax.broadcasted_iota(jnp.int32, middle.shape, dim_index) % 8
    return middle + jnp.where(position == 7, following, 0.0) + jnp.where(position == 0, previous, 0.0)


def pad_axis(array_in, dim_index, before, after):
    config = [(before, after) if place == dim_index else (0, 0) for place in range(array_in.ndim)]
    return jnp.pad(array_in, config)


def extend_axis(padded, dim_index):
    sizes = list(padded.shape)
    length = sizes[dim_index] - 4
    element_count = length // 8
    left_layer = lax.slice_in_dim(padded, 0, length, 8, dim_index)
    own_nodes = lax.slice_in_dim(padded, 2, length + 2, 1, dim_index)
    right_layer = lax.slice_in_dim(padded, 11, length + 4, 8, dim_index)
    single_shape = sizes[:dim_index] + [element_count, 1] + sizes[dim_index + 1:]
    block_shape = sizes[:dim_index] + [element_count, 8] + sizes[dim_index + 1:]
    return jnp.concatenate([left_layer.reshape(single_shape), own_nodes.reshape(block_shape), right_layer.reshape(single_shape)], dim_index + 1)


def contract_axis(blocks, dim_index):
    sizes = list(blocks.shape)
    length = sizes[dim_index] * 8
    merged_shape = sizes[:dim_index] + [length] + sizes[dim_index + 2:]
    left_layer = lax.slice_in_dim(blocks, 0, 1, axis=dim_index + 1)
    own_nodes = lax.slice_in_dim(blocks, 1, 9, axis=dim_index + 1)
    right_layer = lax.slice_in_dim(blocks, 9, 10, axis=dim_index + 1)
    zero_three = jnp.zeros(sizes[:dim_index + 1] + [3] + sizes[dim_index + 2:], blocks.dtype)
    zero_four = jnp.zeros(sizes[:dim_index + 1] + [4] + sizes[dim_index + 2:], blocks.dtype)
    zero_seven = jnp.zeros(sizes[:dim_index + 1] + [7] + sizes[dim_index + 2:], blocks.dtype)
    left_extension_spread = jnp.concatenate([left_layer, zero_seven], dim_index + 1).reshape(merged_shape)
    right_spread = jnp.concatenate([zero_three, right_layer, zero_four], dim_index + 1).reshape(merged_shape)
    right_spread = lax.slice_in_dim(right_spread, 0, length - 4, axis=dim_index)
    return pad_axis(own_nodes.reshape(merged_shape), dim_index, 2, 2) + pad_axis(left_extension_spread, dim_index, 0, 4) + pad_axis(right_spread, dim_index, 8, 0)


def fdm_solve(extended, vectors, values):
    count_x = extended.shape[0]
    count_y = extended.shape[2]
    count_along_depth = extended.shape[4]
    blocks = jnp.transpose(extended, (1, 3, 5, 0, 2, 4)).reshape(10, 10, 10, -1)
    first = jnp.einsum("ame,abce->mbce", vectors[0], blocks, precision=HIGHEST)
    second = jnp.einsum("bne,mbce->mnce", vectors[1], first, precision=HIGHEST)
    third = jnp.einsum("cpe,mnce->mnpe", vectors[2], second, precision=HIGHEST)
    eigenvalue_sum = values[0][:, None, None, :] + values[1][None, :, None, :] + values[2][None, None, :, :]
    scaled = third / eigenvalue_sum
    back_one = jnp.einsum("ame,mnpe->anpe", vectors[0], scaled, precision=HIGHEST)
    back_two = jnp.einsum("bne,anpe->abpe", vectors[1], back_one, precision=HIGHEST)
    result = jnp.einsum("cpe,abpe->abce", vectors[2], back_two, precision=HIGHEST)
    return jnp.transpose(result.reshape(10, 10, 10, count_x, count_y, count_along_depth), (3, 0, 4, 1, 5, 2))


def shared_weight(length, device, devices):
    position = device * length + jnp.arange(length, dtype=jnp.int32)
    shared = ((position % 8 == 7) & (position < length * devices - 1)) | ((position % 8 == 0) & (position > 0))
    return jnp.where(shared, 0.5, 1.0).astype(jnp.float32)


def assemble(field):
    summed = jnp.pad(field, 1)
    for dim_index in range(3):
        summed = pair_add(summed, dim_index)
    return summed


def precondition(residual, vectors, values):
    extended = jnp.pad(residual, 2)
    for dim_index in (0, 2, 4):
        extended = extend_axis(extended, dim_index)
    solved = fdm_solve(extended, vectors, values)
    for dim_index in (4, 2, 0):
        solved = contract_axis(solved, dim_index)
    inner = solved[2:-2, 2:-2, 2:-2]
    return assemble(inner)


def reference(right_side, geometry, element_shape_class, fdm_vectors, fdm_values):
    derivative = jnp.asarray(derivative_table(), jnp.float32)
    weight = (shared_weight(right_side.shape[0], 0, 1)[:, None, None]
              * shared_weight(right_side.shape[1], 0, 1)[None, :, None]
              * shared_weight(right_side.shape[2], 0, 1)[None, None, :])
    flat_class = element_shape_class.reshape(-1).astype(jnp.int32)
    vectors = jnp.transpose(fdm_vectors[flat_class], (1, 2, 3, 0))
    values = jnp.transpose(fdm_values[flat_class], (1, 2, 0))
    solution = jnp.zeros_like(right_side)
    residual = right_side
    direction = jnp.zeros_like(right_side)
    rho_before = jnp.ones((), jnp.float32)
    for number in range(ITERS):
        precond = precondition(residual, vectors, values)
        rho_now = jnp.sum(weight * residual * precond)
        if number == 0:
            direction = precond
        else:
            direction = precond + (rho_now / rho_before) * direction
        image_field = assemble(local_operator(direction, geometry, derivative))
        step_size = rho_now / jnp.sum(weight * direction * image_field)
        solution = solution + step_size * direction
        residual = residual - step_size * image_field
        rho_before = rho_now
    return solution, residual
```

```python
import jax
import jax.numpy as jnp
import numpy as np
from jax import lax
from jax.experimental import pallas as pl
from jax.experimental.pallas import tpu as pltpu
from jax.sharding import PartitionSpec as P

HIGHEST = lax.Precision.HIGHEST
MESH = pl.DeviceIdType.MESH
F32 = jnp.float32
BF16 = jnp.bfloat16
DIRECTIONS = ((1, 0), (-1, 0), (0, 1), (0, -1), (1, 1), (1, -1), (-1, 1), (-1, -1))
STARTS = (0, 16, 32, 48, 64, 72, 80, 88, 96)
ROUNDS = 5


def derivative_table():
    points = np.array(
        [
            -1.0,
            -0.8717401485096066,
            -0.5917001814331423,
            -0.2092992179024789,
            0.2092992179024789,
            0.5917001814331423,
            0.8717401485096066,
            1.0,
        ]
    )
    previous = np.ones(8)
    current = points * 1.0
    for order in range(1, 7):
        following = ((2 * order + 1) * points * current - order * previous) / (order + 1)
        previous = current
        current = following
    spacing = points[:, None] - points[None, :] + np.eye(8)
    off_diagonal = current[:, None] / (current[None, :] * spacing)
    positions = np.arange(8)
    end_values = np.where(positions == 0, -14.0, 0.0) + np.where(positions == 7, 14.0, 0.0)
    return np.where(np.eye(8) > 0, np.eye(8) * end_values[None, :], off_diagonal)


def message_rows(sent):
    own = tuple(range(1, 9))
    for place, (dx, dy) in enumerate(DIRECTIONS):
        xs = sent[dx] if dx else own
        ys = sent[dy] if dy else own
        if dy and not dx:
            pairs = [(x, y) for y in ys for x in xs]
        else:
            pairs = [(x, y) for x in xs for y in ys]
        for number, (x, y) in enumerate(pairs):
            yield STARTS[place] + number, x, y


def node_row(x, y):
    return (x - 1) * 8 + y - 1


def slot_row(x, y):
    return x * 16 + y


def selections():
    gather_from = {1: (7, 8), -1: (2, 1)}
    gather_to = {1: (0, 1), -1: (9, 8)}
    scatter_from = {1: (9, 8), -1: (0, 1)}
    scatter_to = {1: (2, 1), -1: (7, 8)}
    pack_gather = np.zeros((96, 64))
    unpack_gather = np.zeros((160, 160))
    pack_scatter = np.zeros((96, 160))
    unpack_scatter = np.zeros((64, 256))
    for x in range(1, 9):
        for y in range(1, 9):
            unpack_gather[slot_row(x, y), node_row(x, y)] = 1
            unpack_scatter[node_row(x, y), slot_row(x, y)] = 1
    for row, x, y in message_rows(gather_from):
        pack_gather[row, node_row(x, y)] = 1
    for row, x, y in message_rows(gather_to):
        unpack_gather[slot_row(x, y), 64 + row] = 1
    for row, x, y in message_rows(scatter_from):
        pack_scatter[row, slot_row(x, y)] = 1
    for row, x, y in message_rows(scatter_to):
        unpack_scatter[node_row(x, y), 160 + row] = 1
    depth = np.zeros((64, 256))
    for row, lane in enumerate((126, 127, 1, 0)):
        depth[row, lane] = 1
    for row, lane in ((0, 128), (1, 0), (10, 129), (11, 127)):
        depth[16 + row, lane] = 1
    for row, lane in enumerate((129, 127, 128, 0)):
        depth[32 + row, lane] = 1
    for row, lane in ((0, 1), (1, 0), (10, 126), (11, 127)):
        depth[48 + row, lane] = 1
    table = np.zeros((480, 256))
    for start, part in (
        (0, pack_gather),
        (96, unpack_gather),
        (256, pack_scatter),
        (352, unpack_scatter),
        (416, depth),
    ):
        table[start : start + part.shape[0], : part.shape[1]] = part
    return table


def derivative_matrices():
    derivative = derivative_table()
    eye = np.eye(8)
    plane = np.concatenate([np.kron(derivative, eye), np.kron(eye, derivative)], 0)
    deep = np.kron(np.eye(16), derivative)
    table = np.zeros((448, 128))
    table[0:128, :64] = plane
    table[128:192] = plane.T
    table[192:320] = deep.T
    table[320:448] = deep
    return table


def pieces(value):
    high = value.astype(BF16)
    rest = value - high.astype(F32)
    middle = rest.astype(BF16)
    low = (rest - middle.astype(F32)).astype(BF16)
    return low, middle, high


def pick(chooser, value, dims):
    total = None
    for piece in pieces(value):
        part = lax.dot_general(chooser, piece, (dims, ((), ())), preferred_element_type=F32)
        total = part if total is None else total + part
    return total


def place(value, chooser, dims):
    total = None
    for piece in pieces(value):
        part = lax.dot_general(piece, chooser, (dims, ((), ())), preferred_element_type=F32)
        total = part if total is None else total + part
    return total


def kernel(
    counts,
    right_ref,
    geometry_ref,
    class_ref,
    table_ref,
    select_ref,
    derive_ref,
    solution_ref,
    residual_ref,
    deep_send,
    deep_recv,
    plane_send,
    plane_recv,
    first_ref,
    second_ref,
    second_back_ref,
    third_ref,
    third_back_ref,
    inverse_ref,
    sums_plane,
    sums_line,
    deep_sems,
    plane_sems,
    sum_send_sems,
    sum_plane_sems,
    line_send_sems,
    sum_line_sems,
):
    nx, ny, nz = counts
    gx, gy, gz = lax.axis_index("gx"), lax.axis_index("gy"), lax.axis_index("gz")
    plane_size = nx * ny
    me_plane = gx * ny + gy

    deep_recv[...] = jnp.zeros_like(deep_recv)
    plane_recv[...] = jnp.zeros_like(plane_recv)
    deep_send[...] = jnp.zeros_like(deep_send)

    def plane_partner(offset):
        other = lax.rem(me_plane + offset, plane_size)
        return other, (other // ny, lax.rem(other, ny), gz)

    def line_partner(offset):
        other = lax.rem(gz + offset, nz)
        return other, (gx, gy, other)

    barrier = pltpu.get_barrier_semaphore()
    for offset in range(1, plane_size):
        pl.semaphore_signal(
            barrier, inc=1, device_id=plane_partner(offset)[1], device_id_type=MESH
        )
    for offset in range(1, nz):
        pl.semaphore_signal(barrier, inc=1, device_id=line_partner(offset)[1], device_id_type=MESH)
    pl.semaphore_wait(barrier, plane_size + nz - 2)

    def deep_copy(number, step):
        side = 0 if step > 0 else 1
        return pltpu.make_async_remote_copy(
            src_ref=deep_send.at[number],
            dst_ref=deep_recv.at[number, pl.ds(8 * side, 8)],
            send_sem=deep_sems.at[0, number, side],
            recv_sem=deep_sems.at[1, number, side],
            device_id=(gx, gy, gz + step),
            device_id_type=MESH,
        )

    def deep_exists(step):
        return gz + 1 < nz if step > 0 else gz > 0

    def deep_start(number, message):
        deep_send[number, :, 0:64] = message
        for step in (1, -1):
            pl.when(deep_exists(step))(lambda step=step: deep_copy(number, step).start())

    def deep_wait(number):
        for step in (1, -1):
            pl.when(deep_exists(-step))(lambda step=step: deep_copy(number, step).wait_recv())
        return deep_recv[number][:, 0:64]

    def plane_copy(number, at):
        dx, dy = DIRECTIONS[at]
        rows = pl.ds(STARTS[at], STARTS[at + 1] - STARTS[at])
        return pltpu.make_async_remote_copy(
            src_ref=plane_send.at[number, rows],
            dst_ref=plane_recv.at[number, rows],
            send_sem=plane_sems.at[0, number, at],
            recv_sem=plane_sems.at[1, number, at],
            device_id=(gx + dx, gy + dy, gz),
            device_id_type=MESH,
        )

    def plane_exists(dx, dy):
        x, y = gx + dx, gy + dy
        return (x >= 0) & (x < nx) & (y >= 0) & (y < ny)

    def plane_start(number, message):
        plane_send[number] = message
        for at, (dx, dy) in enumerate(DIRECTIONS):
            pl.when(plane_exists(dx, dy))(lambda at=at: plane_copy(number, at).start())

    def plane_wait(number):
        for at, (dx, dy) in enumerate(DIRECTIONS):
            pl.when(plane_exists(-dx, -dy))(lambda at=at: plane_copy(number, at).wait_recv())
        return plane_recv[number]

    rows = lax.broadcasted_iota(jnp.int32, (64, 128), 0)
    lanes = lax.broadcasted_iota(jnp.int32, (64, 128), 1)
    rows_rows = ((1,), (1,))
    plain = ((1,), (0,))
    columns = ((0,), (0,))

    def gather_deep_start(number, field):
        deep_start(number, pick(select_ref[416:424, 0:128], field, rows_rows))

    def gather_deep_end(number, field):
        node = lax.rem(lanes, 8)
        following = jnp.where((node == 7) & (lanes < 127), pltpu.roll(field, 127, 1), 0.0)
        previous = jnp.where((node == 0) & (lanes > 0), pltpu.roll(field, 1, 1), 0.0)
        wide = jnp.concatenate([field + following + previous, jnp.zeros_like(field)], 1)
        return wide + place(deep_wait(number), select_ref[432:448, :], columns)

    def gather_plane_start(number, wide):
        plane_start(number, pick(select_ref[0:96, 0:64], wide, plain))

    def gather_plane_end(number, wide):
        both = jnp.concatenate([wide, plane_wait(number)], 0)
        return pick(select_ref[96:256, 0:160], both, plain)

    def scatter(number, extended):
        plane_start(number, pick(select_ref[256:352, 0:160], extended, plain))
        both = jnp.concatenate([extended, plane_wait(number)], 0)
        wide = pick(select_ref[352:416, :], both, plain)
        deep_start(number, pick(select_ref[448:456, :], wide, rows_rows))
        return wide[:, 0:128] + place(deep_wait(number), select_ref[464:480, 0:128], columns)

    def solve(extended):
        value = jnp.dot(extended, third_ref[...], precision=HIGHEST).reshape(10, 16, 256)
        total = first_ref[0] * value[0][None]
        for a in range(1, 10):
            total = total + first_ref[a] * value[a][None]
        value = total
        total = second_ref[0][None] * value[:, 0:1, :]
        for b in range(1, 10):
            total = total + second_ref[b][None] * value[:, b : b + 1, :]
        value = total * inverse_ref[...]
        total = second_back_ref[0][None] * value[:, 0:1, :]
        for n in range(1, 10):
            total = total + second_back_ref[n][None] * value[:, n : n + 1, :]
        value = total
        total = first_ref[:, 0] * value[0][None]
        for m in range(1, 10):
            total = total + first_ref[:, m] * value[m][None]
        return lax.dot_general(
            total.reshape(160, 256), third_back_ref[...], (rows_rows, ((), ())), precision=HIGHEST
        )

    def local(field):
        slopes = jnp.dot(derive_ref[0:128, 0:64], field, precision=HIGHEST)
        deep = jnp.dot(field, derive_ref[192:320, :], precision=HIGHEST)
        back = jnp.dot(derive_ref[128:192, :], geometry_ref[0:128] * slopes, precision=HIGHEST)
        deep = jnp.dot(geometry_ref[128:192] * deep, derive_ref[320:448, :], precision=HIGHEST)
        return back + deep + geometry_ref[192:256] * field

    def factor(inside, length, device, devices):
        last = (device == devices - 1) & (inside == length - 1)
        first = (device == 0) & (inside == 0)
        node = lax.rem(inside, 8)
        shared = ((node == 7) & ~last) | ((node == 0) & ~first)
        return jnp.where(shared, 0.5, 1.0).astype(F32)

    weight = (
        factor(rows // 8, 8, gx, nx) * factor(lax.rem(rows, 8), 8, gy, ny)
        * factor(lanes, 128, gz, nz)
    )
    right = right_ref[...]
    weighted = weight * right
    gather_deep_start(0, weighted)

    classes = class_ref[...]
    chooser = (lax.broadcasted_iota(jnp.int32, (32, 256), 0) == classes).astype(F32).astype(BF16)
    table = place(table_ref[...], chooser, plain)
    for a in range(10):
        for m in range(10):
            first_ref[a, m] = jnp.broadcast_to(table[a * 10 + m : a * 10 + m + 1], (16, 256))
    second_ref[...] = table[104:264].reshape(10, 16, 256)
    second_back_ref[...] = table[264:424].reshape(10, 16, 256)
    mode = lax.broadcasted_iota(jnp.int32, (1, 256), 1) // 16
    third = jnp.zeros((16, 256), F32)
    level = jnp.zeros((1, 256), F32)
    for p in range(10):
        third = third + jnp.where(mode == p, table[424 + 16 * p : 440 + 16 * p], 0.0)
        level = level + jnp.where(mode == p, table[616 + p : 617 + p], 0.0)

    wide = gather_deep_end(0, weighted)
    gather_plane_start(0, wide)

    for m in range(10):
        inverse_ref[m] = 1.0 / (table[600 + m : 601 + m] + table[584:600] + level)
    node = lax.broadcasted_iota(jnp.int32, (256, 256), 0)
    element = lax.rem(lax.broadcasted_iota(jnp.int32, (256, 256), 1), 16)
    reach = jnp.where(node == 128, -2, node) - 8 * element
    slot = jnp.where(
        reach == -2, 0, jnp.where(reach == 9, 9, jnp.where((reach >= 0) & (reach < 8), reach + 1, -1))
    )
    slot_back = jnp.where(reach == 8, 8, jnp.where(reach == -1, 1, slot))
    spread = jnp.zeros((256, 256), F32)
    spread_back = jnp.zeros((256, 256), F32)
    for c in range(10):
        spread = jnp.where(slot == c, third[c : c + 1], spread)
        spread_back = jnp.where(slot_back == c, third[c : c + 1], spread_back)
    third_ref[...] = spread
    third_back_ref[...] = spread_back

    extended = gather_plane_end(0, wide)
    precond = scatter(1, solve(extended))
    image_local = local(precond)
    gather_deep_start(2, image_local)
    wide = gather_deep_end(2, image_local)
    gather_plane_start(2, wide)
    extended = gather_plane_end(2, wide)
    image = jnp.concatenate(
        [extended[16 * x + 1 : 16 * x + 9, 0:128] for x in range(1, 9)], 0
    )
    again = scatter(3, solve(extended))
    again_local = local(again)

    products = (
        weighted * precond,
        precond * image_local,
        weighted * again,
        weight * image * again,
        precond * again_local,
        again * again_local,
    )
    kind = lax.broadcasted_iota(jnp.int32, (8, 128), 0)
    packed = jnp.zeros((8, 128), F32)
    for number, product in enumerate(products):
        packed = packed + jnp.where(kind == number, jnp.sum(product, 0, keepdims=True), 0.0)

    def sum_copy(buffer, send_sems, recv_sems, offset, mine, partner):
        return pltpu.make_async_remote_copy(
            src_ref=buffer.at[mine],
            dst_ref=buffer.at[mine],
            send_sem=send_sems.at[offset - 1],
            recv_sem=recv_sems.at[mine],
            device_id=partner,
            device_id_type=MESH,
        )

    def sum_wait(buffer, recv_sems, other):
        pltpu.make_async_copy(buffer.at[other], buffer.at[other], recv_sems.at[other]).wait()

    sums_plane[me_plane] = packed
    for offset in range(1, plane_size):
        sum_copy(
            sums_plane, sum_send_sems, sum_plane_sems, offset, me_plane, plane_partner(offset)[1]
        ).start()
    gather_deep_start(4, again_local)
    wide = gather_deep_end(4, again_local)
    gather_plane_start(4, wide)
    for offset in range(1, plane_size):
        sum_wait(sums_plane, sum_plane_sems, plane_partner(offset)[0])
    sums_line[gz] = jnp.sum(sums_plane[...], 0)
    for offset in range(1, nz):
        sum_copy(
            sums_line, line_send_sems, sum_line_sems, offset, gz, line_partner(offset)[1]
        ).start()
    extended = gather_plane_end(4, wide)
    again_image = jnp.concatenate(
        [extended[16 * x + 1 : 16 * x + 9, 0:128] for x in range(1, 9)], 0
    )
    for offset in range(1, nz):
        sum_wait(sums_line, sum_line_sems, line_partner(offset)[0])
    sums = jnp.sum(jnp.sum(sums_line[...], 0), 1, keepdims=True)
    a, b, c, d, e, f = [sums[k : k + 1] for k in range(6)]
    step_one = a / b
    rho = a - step_one * (b + c) + step_one * step_one * d
    stretch = 1.0 + rho / a
    curvature = stretch * stretch * b - stretch * step_one * (d + e) + step_one * step_one * f
    step_two = rho / curvature
    on_precond = step_one + step_two * stretch
    on_again = step_one * step_two
    solution_ref[...] = on_precond * precond - on_again * again
    residual_ref[...] = right - on_precond * image + on_again * again_image

    for number in range(ROUNDS):
        for step in (1, -1):
            pl.when(deep_exists(step))(
                lambda number=number, step=step: deep_copy(number, step).wait_send()
            )
        for at, (dx, dy) in enumerate(DIRECTIONS):
            pl.when(plane_exists(dx, dy))(
                lambda number=number, at=at: plane_copy(number, at).wait_send()
            )
    for offset in range(1, plane_size):
        sum_copy(
            sums_plane, sum_send_sems, sum_plane_sems, offset, me_plane, plane_partner(offset)[1]
        ).wait_send()
    for offset in range(1, nz):
        sum_copy(
            sums_line, line_send_sems, sum_line_sems, offset, gz, line_partner(offset)[1]
        ).wait_send()


def on_device(counts, right_side, geometry, element_shape_class, fdm_vectors, fdm_values):
    nx, ny, nz = counts
    shape = right_side.shape
    classes = jnp.tile(element_shape_class.reshape(1, 16), (1, 16))
    turned = jnp.transpose(fdm_vectors, (1, 2, 3, 0))
    levels = jnp.transpose(fdm_values, (1, 2, 0))

    def padded(part):
        return jnp.pad(part, ((0, 0), (0, 6), (0, 0))).reshape(160, 32)

    table = jnp.concatenate(
        [
            turned[0].reshape(100, 32),
            jnp.zeros((4, 32), F32),
            padded(turned[1]),
            padded(jnp.swapaxes(turned[1], 0, 1)),
            padded(jnp.swapaxes(turned[2], 0, 1)),
            jnp.pad(levels[1], ((0, 6), (0, 0))),
            jnp.pad(levels[0], ((0, 6), (0, 0))),
            jnp.pad(levels[2], ((0, 6), (0, 0))),
        ],
        0,
    )
    vmem = pl.BlockSpec(memory_space=pltpu.VMEM)
    solved, left = pl.pallas_call(
        lambda *refs: kernel(counts, *refs),
        out_shape=(jax.ShapeDtypeStruct((64, 128), F32),) * 2,
        in_specs=[vmem] * 6,
        out_specs=(vmem, vmem),
        scratch_shapes=[
            pltpu.VMEM((ROUNDS, 8, 128), F32),
            pltpu.VMEM((ROUNDS, 16, 128), F32),
            pltpu.VMEM((ROUNDS, 96, 256), F32),
            pltpu.VMEM((ROUNDS, 96, 256), F32),
            pltpu.VMEM((10, 10, 16, 256), F32),
            pltpu.VMEM((10, 16, 256), F32),
            pltpu.VMEM((10, 16, 256), F32),
            pltpu.VMEM((256, 256), F32),
            pltpu.VMEM((256, 256), F32),
            pltpu.VMEM((10, 16, 256), F32),
            pltpu.VMEM((nx * ny, 8, 128), F32),
            pltpu.VMEM((nz, 8, 128), F32),
            pltpu.SemaphoreType.DMA((2, ROUNDS, 2)),
            pltpu.SemaphoreType.DMA((2, ROUNDS, 8)),
            pltpu.SemaphoreType.DMA((nx * ny,)),
            pltpu.SemaphoreType.DMA((nx * ny,)),
            pltpu.SemaphoreType.DMA((nz,)),
            pltpu.SemaphoreType.DMA((nz,)),
        ],
        compiler_params=pltpu.CompilerParams(
            collective_id=0, has_side_effects=True, vmem_limit_bytes=32 * 1024 * 1024
        ),
    )(
        right_side.reshape(64, 128),
        geometry.reshape(256, 128),
        classes,
        table,
        jnp.asarray(selections(), BF16),
        jnp.asarray(derivative_matrices(), F32),
    )
    return solved.reshape(shape), left.reshape(shape)


def solution(mesh):
    counts = tuple(mesh.shape[name] for name in ("gx", "gy", "gz"))
    placed = (P("gx", "gy", "gz"), P(None, "gx", "gy", "gz"), P("gx", "gy", "gz"), P(), P())
    return jax.shard_map(
        lambda *arrays: on_device(counts, *arrays),
        mesh=mesh,
        in_specs=placed,
        out_specs=(P("gx", "gy", "gz"), P("gx", "gy", "gz")),
        check_vma=False,
    )
```

```python
import jax
import jax.numpy as jnp
import numpy as np
from jax import lax
from jax.experimental import pallas as pl
from jax.experimental.pallas import tpu as pltpu
from jax.sharding import PartitionSpec as P

HIGHEST = lax.Precision.HIGHEST
MESH = pl.DeviceIdType.MESH
F32 = jnp.float32
BF16 = jnp.bfloat16
DIRECTIONS = ((1, 0), (-1, 0), (0, 1), (0, -1), (1, 1), (1, -1), (-1, 1), (-1, -1))
STARTS = (0, 16, 32, 48, 64, 72, 80, 88, 96)
ROUNDS = 5


def derivative_table():
    points = np.array(
        [
            -1.0,
            -0.8717401485096066,
            -0.5917001814331423,
            -0.2092992179024789,
            0.2092992179024789,
            0.5917001814331423,
            0.8717401485096066,
            1.0,
        ]
    )
    previous = np.ones(8)
    current = points * 1.0
    for order in range(1, 7):
        following = ((2 * order + 1) * points * current - order * previous) / (order + 1)
        previous = current
        current = following
    spacing = points[:, None] - points[None, :] + np.eye(8)
    off_diagonal = current[:, None] / (current[None, :] * spacing)
    positions = np.arange(8)
    end_values = np.where(positions == 0, -14.0, 0.0) + np.where(positions == 7, 14.0, 0.0)
    return np.where(np.eye(8) > 0, np.eye(8) * end_values[None, :], off_diagonal)


def message_rows(sent):
    own = tuple(range(1, 9))
    for place, (dx, dy) in enumerate(DIRECTIONS):
        xs = sent[dx] if dx else own
        ys = sent[dy] if dy else own
        if dy and not dx:
            pairs = [(x, y) for y in ys for x in xs]
        else:
            pairs = [(x, y) for x in xs for y in ys]
        for number, (x, y) in enumerate(pairs):
            yield STARTS[place] + number, x, y


def node_row(x, y):
    return (x - 1) * 8 + y - 1


def slot_row(x, y):
    return x * 16 + y


def selections():
    gather_from = {1: (7, 8), -1: (2, 1)}
    gather_to = {1: (0, 1), -1: (9, 8)}
    scatter_from = {1: (9, 8), -1: (0, 1)}
    scatter_to = {1: (2, 1), -1: (7, 8)}
    pack_gather = np.zeros((96, 64))
    unpack_gather = np.zeros((160, 160))
    pack_scatter = np.zeros((96, 160))
    unpack_scatter = np.zeros((64, 256))
    for x in range(1, 9):
        for y in range(1, 9):
            unpack_gather[slot_row(x, y), node_row(x, y)] = 1
            unpack_scatter[node_row(x, y), slot_row(x, y)] = 1
    for row, x, y in message_rows(gather_from):
        pack_gather[row, node_row(x, y)] = 1
    for row, x, y in message_rows(gather_to):
        unpack_gather[slot_row(x, y), 64 + row] = 1
    for row, x, y in message_rows(scatter_from):
        pack_scatter[row, slot_row(x, y)] = 1
    for row, x, y in message_rows(scatter_to):
        unpack_scatter[node_row(x, y), 160 + row] = 1
    table = np.zeros((416, 256))
    for start, part in (
        (0, pack_gather),
        (96, unpack_gather),
        (256, pack_scatter),
        (352, unpack_scatter),
    ):
        table[start : start + part.shape[0], : part.shape[1]] = part
    return table


def derivative_matrices():
    derivative = derivative_table()
    eye = np.eye(8)
    plane = np.concatenate([np.kron(derivative, eye), np.kron(eye, derivative)], 0)
    deep = np.kron(np.eye(32), derivative)
    table = np.zeros((704, 256))
    table[0:128, :64] = plane
    table[128:192, :128] = plane.T
    table[192:448] = deep.T
    table[448:704] = deep
    return table


def pieces(value):
    high = value.astype(BF16)
    rest = value - high.astype(F32)
    middle = rest.astype(BF16)
    low = (rest - middle.astype(F32)).astype(BF16)
    return low, middle, high


def pick(chooser, value, dims):
    total = None
    for piece in pieces(value):
        part = lax.dot_general(chooser, piece, (dims, ((), ())), preferred_element_type=F32)
        total = part if total is None else total + part
    return total


def place(value, chooser, dims):
    total = None
    for piece in pieces(value):
        part = lax.dot_general(piece, chooser, (dims, ((), ())), preferred_element_type=F32)
        total = part if total is None else total + part
    return total


def kernel(
    counts,
    right_ref,
    geometry_ref,
    class_ref,
    table_ref,
    select_ref,
    derive_ref,
    solution_ref,
    residual_ref,
    right_recv,
    geometry_recv,
    class_recv,
    wide_geometry,
    plane_send,
    plane_recv,
    first_ref,
    second_ref,
    second_back_ref,
    third_ref,
    third_back_ref,
    inverse_ref,
    sums_plane,
    sums_line,
    deep_sems,
    plane_sems,
    sum_send_sems,
    sum_plane_sems,
    line_send_sems,
    sum_line_sems,
):
    nx, ny, nz = counts
    gx, gy, gz = lax.axis_index("gx"), lax.axis_index("gy"), lax.axis_index("gz")
    plane_size = nx * ny
    me_plane = gx * ny + gy

    right_recv[...] = jnp.zeros_like(right_recv)
    geometry_recv[...] = jnp.zeros_like(geometry_recv)
    class_recv[...] = jnp.zeros_like(class_recv)
    plane_recv[...] = jnp.zeros_like(plane_recv)

    def plane_partner(offset):
        other = lax.rem(me_plane + offset, plane_size)
        return other, (other // ny, lax.rem(other, ny), gz)

    def line_partner(offset):
        other = lax.rem(gz + offset, nz)
        return other, (gx, gy, other)

    barrier = pltpu.get_barrier_semaphore()
    for offset in range(1, plane_size):
        pl.semaphore_signal(
            barrier, inc=1, device_id=plane_partner(offset)[1], device_id_type=MESH
        )
    for offset in range(1, nz):
        pl.semaphore_signal(barrier, inc=1, device_id=line_partner(offset)[1], device_id_type=MESH)
    pl.semaphore_wait(barrier, plane_size + nz - 2)

    inputs = (
        (right_ref, right_recv),
        (class_ref, class_recv),
        (geometry_ref, geometry_recv),
    )

    def deep_copy(number, step):
        side = 0 if step > 0 else 1
        mine, theirs = inputs[number]
        return pltpu.make_async_remote_copy(
            src_ref=mine,
            dst_ref=theirs.at[side],
            send_sem=deep_sems.at[0, number, side],
            recv_sem=deep_sems.at[1, number, side],
            device_id=(gx, gy, gz + step),
            device_id_type=MESH,
        )

    def deep_exists(step):
        return gz + 1 < nz if step > 0 else gz > 0

    def deep_start(number):
        for step in (1, -1):
            pl.when(deep_exists(step))(lambda step=step: deep_copy(number, step).start())

    def deep_wait(number):
        for step in (1, -1):
            pl.when(deep_exists(-step))(lambda step=step: deep_copy(number, step).wait_recv())

    def widen(own, received):
        half = lax.broadcasted_iota(jnp.int32, own.shape, 1) < 64
        return jnp.concatenate([own, jnp.where(half, received[1], received[0])], 1)

    def plane_copy(number, at):
        dx, dy = DIRECTIONS[at]
        rows = pl.ds(STARTS[at], STARTS[at + 1] - STARTS[at])
        return pltpu.make_async_remote_copy(
            src_ref=plane_send.at[number, rows],
            dst_ref=plane_recv.at[number, rows],
            send_sem=plane_sems.at[0, number, at],
            recv_sem=plane_sems.at[1, number, at],
            device_id=(gx + dx, gy + dy, gz),
            device_id_type=MESH,
        )

    def plane_exists(dx, dy):
        x, y = gx + dx, gy + dy
        return (x >= 0) & (x < nx) & (y >= 0) & (y < ny)

    def plane_start(number, message):
        plane_send[number] = message
        for at, (dx, dy) in enumerate(DIRECTIONS):
            pl.when(plane_exists(dx, dy))(lambda at=at: plane_copy(number, at).start())

    def plane_wait(number):
        for at, (dx, dy) in enumerate(DIRECTIONS):
            pl.when(plane_exists(-dx, -dy))(lambda at=at: plane_copy(number, at).wait_recv())
        return plane_recv[number]

    rows = lax.broadcasted_iota(jnp.int32, (64, 128), 0)
    lanes = lax.broadcasted_iota(jnp.int32, (64, 128), 1)
    plain = ((1,), (0,))
    rows_rows = ((1,), (1,))

    def sum_deep(field):
        node = lax.rem(lax.broadcasted_iota(jnp.int32, (64, 256), 1), 8)
        following = jnp.where(node == 7, pltpu.roll(field, 255, 1), 0.0)
        previous = jnp.where(node == 0, pltpu.roll(field, 1, 1), 0.0)
        return field + following + previous

    def gather_plane_start(number, wide):
        plane_start(number, pick(select_ref[0:96, 0:64], wide, plain))

    def gather_plane_end(number, wide):
        both = jnp.concatenate([wide, plane_wait(number)], 0)
        return pick(select_ref[96:256, 0:160], both, plain)

    def scatter(number, extended):
        plane_start(number, pick(select_ref[256:352, 0:160], extended, plain))
        both = jnp.concatenate([extended, plane_wait(number)], 0)
        return pick(select_ref[352:416, :], both, plain)

    def solve(extended):
        value = jnp.dot(extended, third_ref[...], precision=HIGHEST).reshape(10, 16, 256)
        total = first_ref[0] * value[0][None]
        for a in range(1, 10):
            total = total + first_ref[a] * value[a][None]
        value = total
        total = second_ref[0][None] * value[:, 0:1, :]
        for b in range(1, 10):
            total = total + second_ref[b][None] * value[:, b : b + 1, :]
        value = total * inverse_ref[...]
        total = second_back_ref[0][None] * value[:, 0:1, :]
        for n in range(1, 10):
            total = total + second_back_ref[n][None] * value[:, n : n + 1, :]
        value = total
        total = first_ref[:, 0] * value[0][None]
        for m in range(1, 10):
            total = total + first_ref[:, m] * value[m][None]
        return lax.dot_general(
            total.reshape(160, 256), third_back_ref[...], (rows_rows, ((), ())), precision=HIGHEST
        )

    def local(field):
        slopes = jnp.dot(derive_ref[0:128, 0:64], field, precision=HIGHEST)
        deep = jnp.dot(field, derive_ref[192:448, :], precision=HIGHEST)
        back = jnp.dot(
            derive_ref[128:192, 0:128], wide_geometry[0:128] * slopes, precision=HIGHEST
        )
        deep = jnp.dot(wide_geometry[128:192] * deep, derive_ref[448:704, :], precision=HIGHEST)
        return back + deep + wide_geometry[192:256] * field

    def factor(inside, length, device, devices):
        last = (device == devices - 1) & (inside == length - 1)
        first = (device == 0) & (inside == 0)
        node = lax.rem(inside, 8)
        shared = ((node == 7) & ~last) | ((node == 0) & ~first)
        return jnp.where(shared, 0.5, 1.0).astype(F32)

    plane_weight = factor(rows // 8, 8, gx, nx) * factor(lax.rem(rows, 8), 8, gy, ny)
    weight = plane_weight * factor(lanes, 128, gz, nz)
    right = right_ref[...]
    weighted = weight * right
    for number in range(3):
        deep_start(number)
    deep_wait(0)
    wide = jnp.concatenate([plane_weight, plane_weight], 1) * widen(right, right_recv[...])
    gather_plane_start(0, wide)
    deep_wait(1)

    def element_of(shape):
        place_at = lax.rem(lax.broadcasted_iota(jnp.int32, shape, 1), 24)
        return jnp.where(place_at < 20, place_at, place_at - 24)

    source = lax.broadcasted_iota(jnp.int32, (384, 256), 0)
    source = jnp.where(source < 128, source, jnp.where(source < 256, source - 112, source - 272))
    known = jnp.concatenate([class_ref[...], class_recv[1], class_recv[0]], 1).astype(BF16)
    classes = jnp.dot(
        known,
        (source == element_of((384, 256))).astype(F32).astype(BF16),
        preferred_element_type=F32,
    )[0:1]
    kind = lax.broadcasted_iota(jnp.int32, (32, 256), 0).astype(F32)
    chooser = (jnp.abs(kind - classes) < 0.5).astype(F32).astype(BF16)
    table = place(table_ref[...], chooser, plain)
    for a in range(10):
        for m in range(10):
            first_ref[a, m] = jnp.broadcast_to(table[a * 10 + m : a * 10 + m + 1], (16, 256))
    second_ref[...] = table[104:264].reshape(10, 16, 256)
    second_back_ref[...] = table[264:424].reshape(10, 16, 256)
    mode = lax.broadcasted_iota(jnp.int32, (1, 256), 1) // 24
    third = jnp.zeros((16, 256), F32)
    level = jnp.zeros((1, 256), F32)
    for p in range(10):
        third = third + jnp.where(mode == p, table[424 + 16 * p : 440 + 16 * p], 0.0)
        level = level + jnp.where(mode == p, table[616 + p : 617 + p], 0.0)

    for m in range(10):
        inverse_ref[m] = 1.0 / (table[600 + m : 601 + m] + table[584:600] + level)
    node = lax.broadcasted_iota(jnp.int32, (256, 256), 0)
    node = jnp.where(node < 192, node, node - 256)
    element = element_of((256, 256))
    reach = node - 8 * element
    slot = jnp.where(
        reach == -2, 0, jnp.where(reach == 9, 9, jnp.where((reach >= 0) & (reach < 8), reach + 1, -1))
    )
    slot_back = jnp.where(reach == 8, 8, jnp.where(reach == -1, 1, slot))
    inside = (
        (16 * gz + element >= 0)
        & (16 * gz + element < 16 * nz)
        & (128 * gz + node >= 0)
        & (128 * gz + node < 128 * nz)
    )
    slot = jnp.where(inside, slot, -1)
    slot_back = jnp.where(inside, slot_back, -1)
    spread = jnp.zeros((256, 256), F32)
    spread_back = jnp.zeros((256, 256), F32)
    for c in range(10):
        spread = jnp.where(slot == c, third[c : c + 1], spread)
        spread_back = jnp.where(slot_back == c, third[c : c + 1], spread_back)
    third_ref[...] = spread
    third_back_ref[...] = spread_back

    extended = gather_plane_end(0, wide)
    wide_precond = scatter(1, solve(extended))
    deep_wait(2)
    wide_geometry[...] = widen(geometry_ref[...], geometry_recv[...])
    image_local = local(wide_precond)
    wide = sum_deep(image_local)
    gather_plane_start(2, wide)
    extended = gather_plane_end(2, wide)
    image = jnp.concatenate(
        [extended[16 * x + 1 : 16 * x + 9, 0:128] for x in range(1, 9)], 0
    )
    wide_again = scatter(3, solve(extended))
    again_local = local(wide_again)
    precond, again = wide_precond[:, 0:128], wide_again[:, 0:128]

    products = (
        weighted * precond,
        precond * image_local[:, 0:128],
        weighted * again,
        weight * image * again,
        precond * again_local[:, 0:128],
        again * again_local[:, 0:128],
    )
    kind = lax.broadcasted_iota(jnp.int32, (8, 128), 0)
    packed = jnp.zeros((8, 128), F32)
    for number, product in enumerate(products):
        packed = packed + jnp.where(kind == number, jnp.sum(product, 0, keepdims=True), 0.0)

    def sum_copy(buffer, send_sems, recv_sems, offset, mine, partner):
        return pltpu.make_async_remote_copy(
            src_ref=buffer.at[mine],
            dst_ref=buffer.at[mine],
            send_sem=send_sems.at[offset - 1],
            recv_sem=recv_sems.at[mine],
            device_id=partner,
            device_id_type=MESH,
        )

    def sum_wait(buffer, recv_sems, other):
        pltpu.make_async_copy(buffer.at[other], buffer.at[other], recv_sems.at[other]).wait()

    sums_plane[me_plane] = packed
    for offset in range(1, plane_size):
        sum_copy(
            sums_plane, sum_send_sems, sum_plane_sems, offset, me_plane, plane_partner(offset)[1]
        ).start()
    wide = sum_deep(again_local)
    gather_plane_start(4, wide)
    for offset in range(1, plane_size):
        sum_wait(sums_plane, sum_plane_sems, plane_partner(offset)[0])
    sums_line[gz] = jnp.sum(sums_plane[...], 0)
    for offset in range(1, nz):
        sum_copy(
            sums_line, line_send_sems, sum_line_sems, offset, gz, line_partner(offset)[1]
        ).start()
    extended = gather_plane_end(4, wide)
    again_image = jnp.concatenate(
        [extended[16 * x + 1 : 16 * x + 9, 0:128] for x in range(1, 9)], 0
    )
    for offset in range(1, nz):
        sum_wait(sums_line, sum_line_sems, line_partner(offset)[0])
    sums = jnp.sum(jnp.sum(sums_line[...], 0), 1, keepdims=True)
    a, b, c, d, e, f = [sums[k : k + 1] for k in range(6)]
    step_one = a / b
    rho = a - step_one * (b + c) + step_one * step_one * d
    stretch = 1.0 + rho / a
    curvature = stretch * stretch * b - stretch * step_one * (d + e) + step_one * step_one * f
    step_two = rho / curvature
    on_precond = step_one + step_two * stretch
    on_again = step_one * step_two
    solution_ref[...] = on_precond * precond - on_again * again
    residual_ref[...] = right - on_precond * image + on_again * again_image

    for number in range(3):
        for step in (1, -1):
            pl.when(deep_exists(step))(
                lambda number=number, step=step: deep_copy(number, step).wait_send()
            )
    for number in range(ROUNDS):
        for at, (dx, dy) in enumerate(DIRECTIONS):
            pl.when(plane_exists(dx, dy))(
                lambda number=number, at=at: plane_copy(number, at).wait_send()
            )
    for offset in range(1, plane_size):
        sum_copy(
            sums_plane, sum_send_sems, sum_plane_sems, offset, me_plane, plane_partner(offset)[1]
        ).wait_send()
    for offset in range(1, nz):
        sum_copy(
            sums_line, line_send_sems, sum_line_sems, offset, gz, line_partner(offset)[1]
        ).wait_send()


def on_device(counts, right_side, geometry, element_shape_class, fdm_vectors, fdm_values):
    nx, ny, nz = counts
    shape = right_side.shape
    classes = jnp.pad(element_shape_class.reshape(1, 16).astype(F32), ((0, 7), (0, 112)))
    turned = jnp.transpose(fdm_vectors, (1, 2, 3, 0))
    levels = jnp.transpose(fdm_values, (1, 2, 0))

    def padded(part):
        return jnp.pad(part, ((0, 0), (0, 6), (0, 0))).reshape(160, 32)

    table = jnp.concatenate(
        [
            turned[0].reshape(100, 32),
            jnp.zeros((4, 32), F32),
            padded(turned[1]),
            padded(jnp.swapaxes(turned[1], 0, 1)),
            padded(jnp.swapaxes(turned[2], 0, 1)),
            jnp.pad(levels[1], ((0, 6), (0, 0))),
            jnp.pad(levels[0], ((0, 6), (0, 0))),
            jnp.pad(levels[2], ((0, 6), (0, 0))),
        ],
        0,
    )
    vmem = pl.BlockSpec(memory_space=pltpu.VMEM)
    solved, left = pl.pallas_call(
        lambda *refs: kernel(counts, *refs),
        out_shape=(jax.ShapeDtypeStruct((64, 128), F32),) * 2,
        in_specs=[vmem] * 6,
        out_specs=(vmem, vmem),
        scratch_shapes=[
            pltpu.VMEM((2, 64, 128), F32),
            pltpu.VMEM((2, 256, 128), F32),
            pltpu.VMEM((2, 8, 128), F32),
            pltpu.VMEM((256, 256), F32),
            pltpu.VMEM((ROUNDS, 96, 256), F32),
            pltpu.VMEM((ROUNDS, 96, 256), F32),
            pltpu.VMEM((10, 10, 16, 256), F32),
            pltpu.VMEM((10, 16, 256), F32),
            pltpu.VMEM((10, 16, 256), F32),
            pltpu.VMEM((256, 256), F32),
            pltpu.VMEM((256, 256), F32),
            pltpu.VMEM((10, 16, 256), F32),
            pltpu.VMEM((nx * ny, 8, 128), F32),
            pltpu.VMEM((nz, 8, 128), F32),
            pltpu.SemaphoreType.DMA((2, 3, 2)),
            pltpu.SemaphoreType.DMA((2, ROUNDS, 8)),
            pltpu.SemaphoreType.DMA((nx * ny,)),
            pltpu.SemaphoreType.DMA((nx * ny,)),
            pltpu.SemaphoreType.DMA((nz,)),
            pltpu.SemaphoreType.DMA((nz,)),
        ],
        compiler_params=pltpu.CompilerParams(
            collective_id=0, has_side_effects=True, vmem_limit_bytes=32 * 1024 * 1024
        ),
    )(
        right_side.reshape(64, 128),
        geometry.reshape(256, 128),
        classes,
        table,
        jnp.asarray(selections(), BF16),
        jnp.asarray(derivative_matrices(), F32),
    )
    return solved.reshape(shape), left.reshape(shape)


def solution(mesh):
    counts = tuple(mesh.shape[name] for name in ("gx", "gy", "gz"))
    placed = (P("gx", "gy", "gz"), P(None, "gx", "gy", "gz"), P("gx", "gy", "gz"), P(), P())
    return jax.shard_map(
        lambda *arrays: on_device(counts, *arrays),
        mesh=mesh,
        in_specs=placed,
        out_specs=(P("gx", "gy", "gz"), P("gx", "gy", "gz")),
        check_vma=False,
    )
```

```python
import jax
import jax.numpy as jnp
import numpy as np
from jax import lax
from jax.experimental import pallas as pl
from jax.experimental.pallas import tpu as pltpu
from jax.sharding import PartitionSpec as P

MESH = pl.DeviceIdType.MESH
F32 = jnp.float32
BF16 = jnp.bfloat16
DIRECTIONS = ((1, 0), (-1, 0), (0, 1), (0, -1), (1, 1), (1, -1), (-1, 1), (-1, -1))
STARTS = (0, 16, 32, 48, 64, 72, 80, 88, 96)
ROUNDS = 5


def derivative_table():
    points = np.array(
        [
            -1.0,
            -0.8717401485096066,
            -0.5917001814331423,
            -0.2092992179024789,
            0.2092992179024789,
            0.5917001814331423,
            0.8717401485096066,
            1.0,
        ]
    )
    previous = np.ones(8)
    current = points * 1.0
    for order in range(1, 7):
        following = ((2 * order + 1) * points * current - order * previous) / (order + 1)
        previous = current
        current = following
    spacing = points[:, None] - points[None, :] + np.eye(8)
    off_diagonal = current[:, None] / (current[None, :] * spacing)
    positions = np.arange(8)
    end_values = np.where(positions == 0, -14.0, 0.0) + np.where(positions == 7, 14.0, 0.0)
    return np.where(np.eye(8) > 0, np.eye(8) * end_values[None, :], off_diagonal)


def message_rows(sent):
    own = tuple(range(1, 9))
    for place, (dx, dy) in enumerate(DIRECTIONS):
        xs = sent[dx] if dx else own
        ys = sent[dy] if dy else own
        if dy and not dx:
            pairs = [(x, y) for y in ys for x in xs]
        else:
            pairs = [(x, y) for x in xs for y in ys]
        for number, (x, y) in enumerate(pairs):
            yield STARTS[place] + number, x, y


def node_row(x, y):
    return (x - 1) * 8 + y - 1


def slot_row(x, y):
    return x * 16 + y


def selections():
    gather_from = {1: (7, 8), -1: (2, 1)}
    gather_to = {1: (0, 1), -1: (9, 8)}
    scatter_from = {1: (9, 8), -1: (0, 1)}
    scatter_to = {1: (2, 1), -1: (7, 8)}
    pack_gather = np.zeros((96, 128))
    unpack_gather = np.zeros((160, 160))
    pack_scatter = np.zeros((96, 160))
    unpack_scatter = np.zeros((64, 256))
    for x in range(1, 9):
        for y in range(1, 9):
            unpack_gather[slot_row(x, y), node_row(x, y)] = 1
            unpack_scatter[node_row(x, y), slot_row(x, y)] = 1
    for row, x, y in message_rows(gather_from):
        pack_gather[row, [node_row(x, y), 64 + node_row(x, y)]] = 1
    for row, x, y in message_rows(gather_to):
        unpack_gather[slot_row(x, y), 64 + row] = 1
    for row, x, y in message_rows(scatter_from):
        pack_scatter[row, slot_row(x, y)] = 1
    for row, x, y in message_rows(scatter_to):
        unpack_scatter[node_row(x, y), 160 + row] = 1
    derivative = derivative_table()
    eye = np.eye(8)
    plane = np.concatenate([np.kron(derivative, eye), np.kron(eye, derivative)], 0)
    high = np.asarray(np.asarray(plane, BF16), np.float64)
    low = plane - high
    table = np.zeros((608, 256))
    for start, part in (
        (0, pack_gather),
        (96, unpack_gather),
        (256, pack_scatter),
        (352, unpack_scatter),
        (416, np.concatenate([high, high, low], 1)),
        (544, np.concatenate([high.T, low.T], 1)),
    ):
        table[start : start + part.shape[0], : part.shape[1]] = part
    return table


def pieces(value):
    high = value.astype(BF16)
    rest = value - high.astype(F32)
    middle = rest.astype(BF16)
    low = (rest - middle.astype(F32)).astype(BF16)
    return low, middle, high


def halves(value):
    high = value.astype(BF16)
    return high, (value - high.astype(F32)).astype(BF16)


def product(left, right, dims=((1,), (0,))):
    return lax.dot_general(left, right, (dims, ((), ())), preferred_element_type=F32)


def pick(chooser, value):
    high, low = halves(value)
    return product(chooser, low) + product(chooser, high)


def times(value, high_ref, low_ref, dims=((1,), (0,))):
    high, low = halves(value)
    return (
        product(low, high_ref[...], dims)
        + product(high, low_ref[...], dims)
        + product(high, high_ref[...], dims)
    )


def place(value, chooser, dims):
    total = None
    for piece in pieces(value):
        part = lax.dot_general(piece, chooser, (dims, ((), ())), preferred_element_type=F32)
        total = part if total is None else total + part
    return total


def kernel(
    counts,
    right_ref,
    geometry_ref,
    element_ref,
    vectors_ref,
    values_ref,
    select_ref,
    deep_ref,
    result_ref,
    right_recv,
    geometry_recv,
    class_recv,
    wide_geometry,
    class_ref,
    deep_high,
    deep_low,
    plane_send,
    plane_recv,
    first_ref,
    second_ref,
    second_back_ref,
    third_high,
    third_low,
    back_high,
    back_low,
    inverse_ref,
    sums_plane,
    sums_line,
    deep_sems,
    plane_sems,
    sum_send_sems,
    sum_plane_sems,
    line_send_sems,
    sum_line_sems,
):
    nx, ny, nz = counts
    gx, gy, gz = lax.axis_index("gx"), lax.axis_index("gy"), lax.axis_index("gz")
    plane_size = nx * ny
    me_plane = gx * ny + gy

    right_recv[...] = jnp.zeros_like(right_recv)
    geometry_recv[...] = jnp.zeros_like(geometry_recv)
    class_recv[...] = jnp.zeros_like(class_recv)
    plane_recv[...] = jnp.zeros_like(plane_recv)

    def plane_partner(offset):
        other = lax.rem(me_plane + offset, plane_size)
        return other, (other // ny, lax.rem(other, ny), gz)

    def line_partner(offset):
        other = lax.rem(gz + offset, nz)
        return other, (gx, gy, other)

    class_ref[...] = jnp.zeros_like(class_ref)
    class_ref[0:1, 0:16] = element_ref[...].astype(F32)

    barrier = pltpu.get_barrier_semaphore()
    for offset in range(1, plane_size):
        pl.semaphore_signal(
            barrier, inc=1, device_id=plane_partner(offset)[1], device_id_type=MESH
        )
    for offset in range(1, nz):
        pl.semaphore_signal(barrier, inc=1, device_id=line_partner(offset)[1], device_id_type=MESH)
    pl.semaphore_wait(barrier, plane_size + nz - 2)

    inputs = (
        (right_ref, right_recv),
        (class_ref, class_recv),
        (geometry_ref, geometry_recv),
    )

    def deep_copy(number, step):
        side = 0 if step > 0 else 1
        mine, theirs = inputs[number]
        return pltpu.make_async_remote_copy(
            src_ref=mine,
            dst_ref=theirs.at[side],
            send_sem=deep_sems.at[0, number, side],
            recv_sem=deep_sems.at[1, number, side],
            device_id=(gx, gy, gz + step),
            device_id_type=MESH,
        )

    def deep_exists(step):
        return gz + 1 < nz if step > 0 else gz > 0

    def deep_start(number):
        for step in (1, -1):
            pl.when(deep_exists(step))(lambda step=step: deep_copy(number, step).start())

    def deep_wait(number):
        for step in (1, -1):
            pl.when(deep_exists(-step))(lambda step=step: deep_copy(number, step).wait_recv())

    def widen(own, received):
        half = lax.broadcasted_iota(jnp.int32, own.shape, 1) < 64
        return jnp.concatenate([own, jnp.where(half, received[1], received[0])], 1)

    def plane_copy(number, at):
        dx, dy = DIRECTIONS[at]
        rows = pl.ds(STARTS[at], STARTS[at + 1] - STARTS[at])
        return pltpu.make_async_remote_copy(
            src_ref=plane_send.at[number, rows],
            dst_ref=plane_recv.at[number, rows],
            send_sem=plane_sems.at[0, number, at],
            recv_sem=plane_sems.at[1, number, at],
            device_id=(gx + dx, gy + dy, gz),
            device_id_type=MESH,
        )

    def plane_exists(dx, dy):
        x, y = gx + dx, gy + dy
        return (x >= 0) & (x < nx) & (y >= 0) & (y < ny)

    def plane_start(number, message):
        plane_send[number] = message
        for at, (dx, dy) in enumerate(DIRECTIONS):
            pl.when(plane_exists(dx, dy))(lambda at=at: plane_copy(number, at).start())

    def plane_wait(number):
        for at, (dx, dy) in enumerate(DIRECTIONS):
            pl.when(plane_exists(-dx, -dy))(lambda at=at: plane_copy(number, at).wait_recv())
        return plane_recv[number]

    rows = lax.broadcasted_iota(jnp.int32, (64, 128), 0)
    lanes = lax.broadcasted_iota(jnp.int32, (64, 128), 1)
    plain = ((1,), (0,))
    rows_rows = ((1,), (1,))

    def sum_deep(field):
        node = lax.rem(lax.broadcasted_iota(jnp.int32, (64, 256), 1), 8)
        following = jnp.where(node == 7, pltpu.roll(field, 255, 1), 0.0)
        previous = jnp.where(node == 0, pltpu.roll(field, 1, 1), 0.0)
        return field + following + previous

    def gather_plane_start(number, wide):
        plane_start(number, product(select_ref[0:96, 0:128], jnp.concatenate(halves(wide), 0)))

    def gather_plane_end(number, wide):
        both = jnp.concatenate([wide, plane_wait(number)], 0)
        return pick(select_ref[96:256, 0:160], both)

    def scatter(number, extended):
        plane_start(number, pick(select_ref[256:352, 0:160], extended))
        both = jnp.concatenate([extended, plane_wait(number)], 0)
        return pick(select_ref[352:416, :], both)

    def solve(extended):
        value = times(extended, third_high, third_low).reshape(10, 16, 256)
        total = first_ref[0] * value[0][None]
        for a in range(1, 10):
            total = total + first_ref[a] * value[a][None]
        value = total
        total = second_ref[0][None] * value[:, 0:1, :]
        for b in range(1, 10):
            total = total + second_ref[b][None] * value[:, b : b + 1, :]
        value = total * inverse_ref[...]
        total = second_back_ref[0][None] * value[:, 0:1, :]
        for n in range(1, 10):
            total = total + second_back_ref[n][None] * value[:, n : n + 1, :]
        value = total
        total = first_ref[:, 0] * value[0][None]
        for m in range(1, 10):
            total = total + first_ref[:, m] * value[m][None]
        return times(total.reshape(160, 256), back_high, back_low, rows_rows)

    def slopes_of(field):
        high, low = halves(field)
        slopes = product(select_ref[416:544, 0:192], jnp.concatenate([high, low, high], 0))
        return slopes, times(field, deep_high, deep_low)

    def local(field, slopes, deep):
        high, low = halves(wide_geometry[0:128] * slopes)
        back = (
            product(select_ref[544:608, 0:128], low)
            + product(select_ref[544:608, 128:256], high)
            + product(select_ref[544:608, 0:128], high)
        )
        deep = times(wide_geometry[128:192] * deep, deep_high, deep_low, rows_rows)
        return back + deep + wide_geometry[192:256] * field

    def factor(inside, length, device, devices):
        last = (device == devices - 1) & (inside == length - 1)
        first = (device == 0) & (inside == 0)
        node = lax.rem(inside, 8)
        shared = ((node == 7) & ~last) | ((node == 0) & ~first)
        return jnp.where(shared, 0.5, 1.0).astype(F32)

    plane_weight = factor(rows // 8, 8, gx, nx) * factor(lax.rem(rows, 8), 8, gy, ny)
    weight = plane_weight * factor(lanes, 128, gz, nz)
    right = right_ref[...]
    weighted = weight * right
    for number in range(3):
        deep_start(number)

    blank = jnp.zeros((6, 32), F32)
    groups = (
        [vectors_ref[a, :, 0, :] for a in range(10)]
        + [vectors_ref[b, :, 1, :] for b in range(10)]
        + [vectors_ref[:, n, 1, :] for n in range(10)]
        + [vectors_ref[:, p, 2, :] for p in range(10)]
        + [values_ref[:, d, :] for d in (1, 0, 2)]
    )
    entries = jnp.concatenate([part for group in groups for part in (group, blank)], 0)
    corner = lax.broadcasted_iota(jnp.int32, (256, 256), 0) // 8
    along = lax.broadcasted_iota(jnp.int32, (256, 256), 1) // 8
    high, low = halves(jnp.where(corner == along, jnp.concatenate([deep_ref[...]] * 32, 0), 0.0))
    deep_high[...] = high
    deep_low[...] = low
    deep_wait(0)
    wide = jnp.concatenate([plane_weight, plane_weight], 1) * widen(right, right_recv[...])
    gather_plane_start(0, wide)
    deep_wait(1)

    def element_of(shape):
        place_at = lax.rem(lax.broadcasted_iota(jnp.int32, shape, 1), 24)
        return jnp.where(place_at < 20, place_at, place_at - 24)

    source = lax.broadcasted_iota(jnp.int32, (384, 256), 0)
    source = jnp.where(source < 128, source, jnp.where(source < 256, source - 112, source - 272))
    known = jnp.concatenate([class_ref[...], class_recv[1], class_recv[0]], 1).astype(BF16)
    classes = jnp.dot(
        known,
        (source == element_of((384, 256))).astype(F32).astype(BF16),
        preferred_element_type=F32,
    )[0:1]
    kind = lax.broadcasted_iota(jnp.int32, (32, 256), 0).astype(F32)
    chooser = (jnp.abs(kind - classes) < 0.5).astype(F32).astype(BF16)
    table = place(entries, chooser, plain)
    for a in range(10):
        for m in range(10):
            first_ref[a, m] = jnp.broadcast_to(table[a * 16 + m : a * 16 + m + 1], (16, 256))
    second_ref[...] = table[160:320].reshape(10, 16, 256)
    second_back_ref[...] = table[320:480].reshape(10, 16, 256)
    mode = lax.broadcasted_iota(jnp.int32, (1, 256), 1) // 24
    third = jnp.zeros((16, 256), F32)
    level = jnp.zeros((1, 256), F32)
    for p in range(10):
        third = third + jnp.where(mode == p, table[480 + 16 * p : 496 + 16 * p], 0.0)
        level = level + jnp.where(mode == p, table[672 + p : 673 + p], 0.0)

    for m in range(10):
        inverse_ref[m] = 1.0 / (table[656 + m : 657 + m] + table[640:656] + level)
    node = lax.broadcasted_iota(jnp.int32, (256, 256), 0)
    node = jnp.where(node < 192, node, node - 256)
    element = element_of((256, 256))
    reach = node - 8 * element
    slot = jnp.where(
        reach == -2, 0, jnp.where(reach == 9, 9, jnp.where((reach >= 0) & (reach < 8), reach + 1, -1))
    )
    slot_back = jnp.where(reach == 8, 8, jnp.where(reach == -1, 1, slot))
    inside = (
        (16 * gz + element >= 0)
        & (16 * gz + element < 16 * nz)
        & (128 * gz + node >= 0)
        & (128 * gz + node < 128 * nz)
    )
    slot = jnp.where(inside, slot, -1)
    slot_back = jnp.where(inside, slot_back, -1)
    spread = jnp.zeros((256, 256), F32)
    spread_back = jnp.zeros((256, 256), F32)
    for c in range(10):
        spread = jnp.where(slot == c, third[c : c + 1], spread)
        spread_back = jnp.where(slot_back == c, third[c : c + 1], spread_back)
    third_high[...], third_low[...] = halves(spread)
    back_high[...], back_low[...] = halves(spread_back)

    extended = gather_plane_end(0, wide)
    wide_precond = scatter(1, solve(extended))
    deep_wait(2)
    wide_geometry[...] = widen(geometry_ref[...], geometry_recv[...])
    image_local = local(wide_precond, *slopes_of(wide_precond))
    wide = sum_deep(image_local)
    gather_plane_start(2, wide)
    extended = gather_plane_end(2, wide)
    image = jnp.concatenate(
        [extended[16 * x + 1 : 16 * x + 9, 0:128] for x in range(1, 9)], 0
    )
    wide_again = scatter(3, solve(extended))
    slopes, deep = slopes_of(wide_again)
    precond, again = wide_precond[:, 0:128], wide_again[:, 0:128]

    own = geometry_ref[...]
    energy = (
        own[0:64] * slopes[0:64, 0:128] * slopes[0:64, 0:128]
        + own[64:128] * slopes[64:128, 0:128] * slopes[64:128, 0:128]
        + own[128:192] * deep[:, 0:128] * deep[:, 0:128]
        + own[192:256] * again * again
    )
    products = (
        weighted * precond,
        precond * image_local[:, 0:128],
        weighted * again,
        weight * image * again,
        energy,
    )
    kind = lax.broadcasted_iota(jnp.int32, (8, 128), 0)
    packed = jnp.zeros((8, 128), F32)
    for number, entry in enumerate(products):
        packed = packed + jnp.where(kind == number, jnp.sum(entry, 0, keepdims=True), 0.0)

    def sum_copy(buffer, send_sems, recv_sems, offset, mine, partner):
        return pltpu.make_async_remote_copy(
            src_ref=buffer.at[mine],
            dst_ref=buffer.at[mine],
            send_sem=send_sems.at[offset - 1],
            recv_sem=recv_sems.at[mine],
            device_id=partner,
            device_id_type=MESH,
        )

    def sum_wait(buffer, recv_sems, other):
        pltpu.make_async_copy(buffer.at[other], buffer.at[other], recv_sems.at[other]).wait()

    sums_plane[me_plane] = packed
    for offset in range(1, plane_size):
        sum_copy(
            sums_plane, sum_send_sems, sum_plane_sems, offset, me_plane, plane_partner(offset)[1]
        ).start()
    wide = sum_deep(local(wide_again, slopes, deep))
    gather_plane_start(4, wide)
    for offset in range(1, plane_size):
        sum_wait(sums_plane, sum_plane_sems, plane_partner(offset)[0])
    sums_line[gz] = jnp.sum(sums_plane[...], 0)
    for offset in range(1, nz):
        sum_copy(
            sums_line, line_send_sems, sum_line_sems, offset, gz, line_partner(offset)[1]
        ).start()
    extended = gather_plane_end(4, wide)
    again_image = jnp.concatenate(
        [extended[16 * x + 1 : 16 * x + 9, 0:128] for x in range(1, 9)], 0
    )
    for offset in range(1, nz):
        sum_wait(sums_line, sum_line_sems, line_partner(offset)[0])
    sums = jnp.sum(jnp.sum(sums_line[...], 0), 1, keepdims=True)
    a, b, c, d, f = [sums[k : k + 1] for k in range(5)]
    step_one = a / b
    rho = a - step_one * (b + c) + step_one * step_one * d
    stretch = 1.0 + rho / a
    curvature = stretch * stretch * b - 2.0 * stretch * step_one * d + step_one * step_one * f
    step_two = rho / curvature
    on_precond = step_one + step_two * stretch
    on_again = step_one * step_two
    result_ref[0] = on_precond * precond - on_again * again
    result_ref[1] = right - on_precond * image + on_again * again_image

    for number in range(3):
        for step in (1, -1):
            pl.when(deep_exists(step))(
                lambda number=number, step=step: deep_copy(number, step).wait_send()
            )
    for number in range(ROUNDS):
        for at, (dx, dy) in enumerate(DIRECTIONS):
            pl.when(plane_exists(dx, dy))(
                lambda number=number, at=at: plane_copy(number, at).wait_send()
            )
    for offset in range(1, plane_size):
        sum_copy(
            sums_plane, sum_send_sems, sum_plane_sems, offset, me_plane, plane_partner(offset)[1]
        ).wait_send()
    for offset in range(1, nz):
        sum_copy(
            sums_line, line_send_sems, sum_line_sems, offset, gz, line_partner(offset)[1]
        ).wait_send()


def on_device(counts, right_side, geometry, element_shape_class, fdm_vectors, fdm_values):
    nx, ny, nz = counts
    shape = right_side.shape
    vmem = pl.BlockSpec(memory_space=pltpu.VMEM)
    result = pl.pallas_call(
        lambda *refs: kernel(counts, *refs),
        out_shape=jax.ShapeDtypeStruct((2, 64, 128), F32),
        in_specs=[vmem] * 7,
        out_specs=vmem,
        scratch_shapes=[
            pltpu.VMEM((2, 64, 128), F32),
            pltpu.VMEM((2, 256, 128), F32),
            pltpu.VMEM((2, 8, 128), F32),
            pltpu.VMEM((256, 256), F32),
            pltpu.VMEM((8, 128), F32),
            pltpu.VMEM((256, 256), BF16),
            pltpu.VMEM((256, 256), BF16),
            pltpu.VMEM((ROUNDS, 96, 256), F32),
            pltpu.VMEM((ROUNDS, 96, 256), F32),
            pltpu.VMEM((10, 10, 16, 256), F32),
            pltpu.VMEM((10, 16, 256), F32),
            pltpu.VMEM((10, 16, 256), F32),
            pltpu.VMEM((256, 256), BF16),
            pltpu.VMEM((256, 256), BF16),
            pltpu.VMEM((256, 256), BF16),
            pltpu.VMEM((256, 256), BF16),
            pltpu.VMEM((10, 16, 256), F32),
            pltpu.VMEM((nx * ny, 8, 128), F32),
            pltpu.VMEM((nz, 8, 128), F32),
            pltpu.SemaphoreType.DMA((2, 3, 2)),
            pltpu.SemaphoreType.DMA((2, ROUNDS, 8)),
            pltpu.SemaphoreType.DMA((nx * ny,)),
            pltpu.SemaphoreType.DMA((nx * ny,)),
            pltpu.SemaphoreType.DMA((nz,)),
            pltpu.SemaphoreType.DMA((nz,)),
        ],
        compiler_params=pltpu.CompilerParams(
            collective_id=0, has_side_effects=True, vmem_limit_bytes=32 * 1024 * 1024
        ),
    )(
        right_side.reshape(64, 128),
        geometry.reshape(256, 128),
        element_shape_class.reshape(1, 16),
        jnp.transpose(fdm_vectors, (2, 3, 1, 0)),
        jnp.transpose(fdm_values, (2, 1, 0)),
        jnp.asarray(selections(), BF16),
        jnp.asarray(np.tile(derivative_table().T, (1, 32)), F32),
    )
    return result[0].reshape(shape), result[1].reshape(shape)


def solution(mesh):
    counts = tuple(mesh.shape[name] for name in ("gx", "gy", "gz"))
    placed = (P("gx", "gy", "gz"), P(None, "gx", "gy", "gz"), P("gx", "gy", "gz"), P(), P())
    return jax.shard_map(
        lambda *arrays: on_device(counts, *arrays),
        mesh=mesh,
        in_specs=placed,
        out_specs=(P("gx", "gy", "gz"), P("gx", "gy", "gz")),
        check_vma=False,
    )
```

```python
import jax
import jax.numpy as jnp
import numpy as np
from jax import lax
from jax.experimental import pallas as pl
from jax.experimental.pallas import tpu as pltpu
from jax.sharding import PartitionSpec as P

MESH = pl.DeviceIdType.MESH
F32 = jnp.float32
BF16 = jnp.bfloat16
DIRECTIONS = ((1, 0), (-1, 0), (0, 1), (0, -1), (1, 1), (1, -1), (-1, 1), (-1, -1))
STARTS = (0, 16, 32, 48, 64, 72, 80, 88, 96)
ROUNDS = 5
LEVELS = (0, 1, -1)


def derivative_table():
    points = np.array(
        [
            -1.0,
            -0.8717401485096066,
            -0.5917001814331423,
            -0.2092992179024789,
            0.2092992179024789,
            0.5917001814331423,
            0.8717401485096066,
            1.0,
        ]
    )
    previous = np.ones(8)
    current = points * 1.0
    for order in range(1, 7):
        following = ((2 * order + 1) * points * current - order * previous) / (order + 1)
        previous = current
        current = following
    spacing = points[:, None] - points[None, :] + np.eye(8)
    off_diagonal = current[:, None] / (current[None, :] * spacing)
    positions = np.arange(8)
    end_values = np.where(positions == 0, -14.0, 0.0) + np.where(positions == 7, 14.0, 0.0)
    return np.where(np.eye(8) > 0, np.eye(8) * end_values[None, :], off_diagonal)


def message_rows(sent):
    own = tuple(range(1, 9))
    for place, (dx, dy) in enumerate(DIRECTIONS):
        xs = sent[dx] if dx else own
        ys = sent[dy] if dy else own
        if dy and not dx:
            pairs = [(x, y) for y in ys for x in xs]
        else:
            pairs = [(x, y) for x in xs for y in ys]
        for number, (x, y) in enumerate(pairs):
            yield STARTS[place] + number, x, y


def node_row(x, y):
    return (x - 1) * 8 + y - 1


def slot_row(x, y):
    return x * 16 + y


def selections():
    gather_from = {1: (7, 8), -1: (2, 1)}
    gather_to = {1: (0, 1), -1: (9, 8)}
    scatter_from = {1: (9, 8), -1: (0, 1)}
    scatter_to = {1: (2, 1), -1: (7, 8)}
    pack_gather = np.zeros((96, 128))
    unpack_gather = np.zeros((160, 160))
    pack_scatter = np.zeros((96, 160))
    unpack_scatter = np.zeros((64, 256))
    for x in range(1, 9):
        for y in range(1, 9):
            unpack_gather[slot_row(x, y), node_row(x, y)] = 1
            unpack_scatter[node_row(x, y), slot_row(x, y)] = 1
    for row, x, y in message_rows(gather_from):
        pack_gather[row, [node_row(x, y), 64 + node_row(x, y)]] = 1
    for row, x, y in message_rows(gather_to):
        unpack_gather[slot_row(x, y), 64 + row] = 1
    for row, x, y in message_rows(scatter_from):
        pack_scatter[row, slot_row(x, y)] = 1
    for row, x, y in message_rows(scatter_to):
        unpack_scatter[node_row(x, y), 160 + row] = 1
    derivative = derivative_table()
    eye = np.eye(8)
    plane = np.concatenate([np.kron(derivative, eye), np.kron(eye, derivative)], 0)
    high = np.asarray(np.asarray(plane, BF16), np.float64)
    low = plane - high
    table = np.zeros((608, 256))
    for start, part in (
        (0, pack_gather),
        (96, unpack_gather),
        (256, pack_scatter),
        (352, unpack_scatter),
        (416, np.concatenate([high, high, low], 1)),
        (544, np.concatenate([high.T, low.T], 1)),
    ):
        table[start : start + part.shape[0], : part.shape[1]] = part
    return table


def pieces(value):
    high = value.astype(BF16)
    rest = value - high.astype(F32)
    middle = rest.astype(BF16)
    low = (rest - middle.astype(F32)).astype(BF16)
    return low, middle, high


def halves(value):
    high = value.astype(BF16)
    return high, (value - high.astype(F32)).astype(BF16)


def product(left, right, dims=((1,), (0,))):
    return lax.dot_general(left, right, (dims, ((), ())), preferred_element_type=F32)


def pick(chooser, value):
    high, low = halves(value)
    return product(chooser, low) + product(chooser, high)


def times(value, high_ref, low_ref, dims=((1,), (0,))):
    high, low = halves(value)
    return (
        product(low, high_ref[...], dims)
        + product(high, low_ref[...], dims)
        + product(high, high_ref[...], dims)
    )


def place(value, chooser, dims):
    total = None
    for piece in pieces(value):
        part = lax.dot_general(piece, chooser, (dims, ((), ())), preferred_element_type=F32)
        total = part if total is None else total + part
    return total


def kernel(
    counts,
    right_hbm,
    geometry_hbm,
    element_hbm,
    vectors_hbm,
    values_hbm,
    select_hbm,
    deep_hbm,
    result_ref,
    right_ref,
    geometry_ref,
    element_ref,
    vectors_ref,
    values_ref,
    select_ref,
    deep_ref,
    start_send,
    start_recv,
    right_recv,
    geometry_recv,
    class_recv,
    wide_geometry,
    class_ref,
    deep_high,
    deep_low,
    plane_send,
    plane_recv,
    first_ref,
    second_ref,
    second_back_ref,
    third_high,
    third_low,
    back_high,
    back_low,
    inverse_ref,
    sums_plane,
    sums_line,
    load_sems,
    start_sems,
    deep_sems,
    plane_sems,
    sum_send_sems,
    sum_plane_sems,
    line_send_sems,
    sum_line_sems,
):
    nx, ny, nz = counts
    gx, gy, gz = lax.axis_index("gx"), lax.axis_index("gy"), lax.axis_index("gz")
    plane_size = nx * ny
    me_plane = gx * ny + gy

    loads = [
        pltpu.make_async_copy(source, target, load_sems.at[number])
        for number, (source, target) in enumerate(
            (
                (right_hbm, right_ref),
                (select_hbm, select_ref),
                (element_hbm, element_ref),
                (vectors_hbm, vectors_ref),
                (values_hbm, values_ref),
                (deep_hbm, deep_ref),
                (geometry_hbm, geometry_ref),
            )
        )
    ]
    for load in loads:
        load.start()

    start_recv[...] = jnp.zeros_like(start_recv)
    right_recv[...] = jnp.zeros_like(right_recv)
    geometry_recv[...] = jnp.zeros_like(geometry_recv)
    class_recv[...] = jnp.zeros_like(class_recv)
    plane_recv[...] = jnp.zeros_like(plane_recv)

    def plane_partner(offset):
        other = lax.rem(me_plane + offset, plane_size)
        return other, (other // ny, lax.rem(other, ny), gz)

    def line_partner(offset):
        other = lax.rem(gz + offset, nz)
        return other, (gx, gy, other)

    class_ref[...] = jnp.zeros_like(class_ref)

    def exists(dx, dy, dz):
        x, y, z = gx + dx, gy + dy, gz + dz
        return (x >= 0) & (x < nx) & (y >= 0) & (y < ny) & (z >= 0) & (z < nz)

    barrier = pltpu.get_barrier_semaphore()
    for offset in range(1, plane_size):
        pl.semaphore_signal(
            barrier, inc=1, device_id=plane_partner(offset)[1], device_id_type=MESH
        )
    for offset in range(1, nz):
        pl.semaphore_signal(barrier, inc=1, device_id=line_partner(offset)[1], device_id_type=MESH)
    slanted = [(dx, dy, dz) for dz in (1, -1) for dx, dy in DIRECTIONS]
    partners = plane_size + nz - 2
    for step in slanted:
        pl.when(exists(*step))(
            lambda step=step: pl.semaphore_signal(
                barrier,
                inc=1,
                device_id=(gx + step[0], gy + step[1], gz + step[2]),
                device_id_type=MESH,
            )
        )
        partners = partners + exists(*step).astype(jnp.int32)
    pl.semaphore_wait(barrier, partners)

    inputs = (
        (right_hbm, right_recv),
        (class_ref, class_recv),
        (geometry_hbm, geometry_recv),
    )

    def deep_copy(number, step):
        side = 0 if step > 0 else 1
        mine, theirs = inputs[number]
        return pltpu.make_async_remote_copy(
            src_ref=mine,
            dst_ref=theirs.at[side],
            send_sem=deep_sems.at[0, number, side],
            recv_sem=deep_sems.at[1, number, side],
            device_id=(gx, gy, gz + step),
            device_id_type=MESH,
        )

    def deep_exists(step):
        return gz + 1 < nz if step > 0 else gz > 0

    def deep_start(number):
        for step in (1, -1):
            pl.when(deep_exists(step))(lambda step=step: deep_copy(number, step).start())

    def deep_wait(number):
        for step in (1, -1):
            pl.when(deep_exists(-step))(lambda step=step: deep_copy(number, step).wait_recv())

    def widen(own, received):
        half = lax.broadcasted_iota(jnp.int32, own.shape, 1) < 64
        return jnp.concatenate([own, jnp.where(half, received[1], received[0])], 1)

    def plane_copy(number, at):
        dx, dy = DIRECTIONS[at]
        rows = pl.ds(STARTS[at], STARTS[at + 1] - STARTS[at])
        return pltpu.make_async_remote_copy(
            src_ref=plane_send.at[number, rows],
            dst_ref=plane_recv.at[number, rows],
            send_sem=plane_sems.at[0, number, at],
            recv_sem=plane_sems.at[1, number, at],
            device_id=(gx + dx, gy + dy, gz),
            device_id_type=MESH,
        )

    def plane_exists(dx, dy):
        return exists(dx, dy, 0)

    def start_copy(level, at):
        dx, dy = DIRECTIONS[at]
        rows = pl.ds(STARTS[at], STARTS[at + 1] - STARTS[at])
        return pltpu.make_async_remote_copy(
            src_ref=start_send.at[rows],
            dst_ref=start_recv.at[level, rows],
            send_sem=start_sems.at[0, level, at],
            recv_sem=start_sems.at[1, level, at],
            device_id=(gx + dx, gy + dy, gz + LEVELS[level]),
            device_id_type=MESH,
        )

    def start_each(action, sign):
        for level, dz in enumerate(LEVELS):
            for at, (dx, dy) in enumerate(DIRECTIONS):
                pl.when(exists(sign * dx, sign * dy, sign * dz))(
                    lambda level=level, at=at: action(start_copy(level, at))
                )

    def plane_start(number, message):
        plane_send[number] = message
        for at, (dx, dy) in enumerate(DIRECTIONS):
            pl.when(plane_exists(dx, dy))(lambda at=at: plane_copy(number, at).start())

    def plane_wait(number):
        for at, (dx, dy) in enumerate(DIRECTIONS):
            pl.when(plane_exists(-dx, -dy))(lambda at=at: plane_copy(number, at).wait_recv())
        return plane_recv[number]

    rows = lax.broadcasted_iota(jnp.int32, (64, 128), 0)
    lanes = lax.broadcasted_iota(jnp.int32, (64, 128), 1)
    plain = ((1,), (0,))
    rows_rows = ((1,), (1,))

    def sum_deep(field):
        node = lax.rem(lax.broadcasted_iota(jnp.int32, (64, 256), 1), 8)
        following = jnp.where(node == 7, pltpu.roll(field, 255, 1), 0.0)
        previous = jnp.where(node == 0, pltpu.roll(field, 1, 1), 0.0)
        return field + following + previous

    def gather_plane_start(number, wide):
        plane_start(number, product(select_ref[0:96, 0:128], jnp.concatenate(halves(wide), 0)))

    def gather_plane_end(wide, received):
        both = jnp.concatenate([wide, received], 0)
        return pick(select_ref[96:256, 0:160], both)

    def scatter(number, extended):
        plane_start(number, pick(select_ref[256:352, 0:160], extended))
        both = jnp.concatenate([extended, plane_wait(number)], 0)
        return pick(select_ref[352:416, :], both)

    def solve(extended):
        value = times(extended, third_high, third_low).reshape(10, 16, 256)
        total = first_ref[0] * value[0][None]
        for a in range(1, 10):
            total = total + first_ref[a] * value[a][None]
        value = total
        total = second_ref[0][None] * value[:, 0:1, :]
        for b in range(1, 10):
            total = total + second_ref[b][None] * value[:, b : b + 1, :]
        value = total * inverse_ref[...]
        total = second_back_ref[0][None] * value[:, 0:1, :]
        for n in range(1, 10):
            total = total + second_back_ref[n][None] * value[:, n : n + 1, :]
        value = total
        total = first_ref[:, 0] * value[0][None]
        for m in range(1, 10):
            total = total + first_ref[:, m] * value[m][None]
        return times(total.reshape(160, 256), back_high, back_low, rows_rows)

    def slopes_of(field):
        high, low = halves(field)
        slopes = product(select_ref[416:544, 0:192], jnp.concatenate([high, low, high], 0))
        return slopes, times(field, deep_high, deep_low)

    def local(field, slopes, deep):
        high, low = halves(wide_geometry[0:128] * slopes)
        back = (
            product(select_ref[544:608, 0:128], low)
            + product(select_ref[544:608, 128:256], high)
            + product(select_ref[544:608, 0:128], high)
        )
        deep = times(wide_geometry[128:192] * deep, deep_high, deep_low, rows_rows)
        return back + deep + wide_geometry[192:256] * field

    def factor(inside, length, device, devices):
        last = (device == devices - 1) & (inside == length - 1)
        first = (device == 0) & (inside == 0)
        node = lax.rem(inside, 8)
        shared = ((node == 7) & ~last) | ((node == 0) & ~first)
        return jnp.where(shared, 0.5, 1.0).astype(F32)

    plane_weight = factor(rows // 8, 8, gx, nx) * factor(lax.rem(rows, 8), 8, gy, ny)
    weight = plane_weight * factor(lanes, 128, gz, nz)
    deep_start(0)
    loads[0].wait()
    loads[1].wait()
    right = right_ref[...]
    weighted = weight * right
    start_send[...] = product(
        select_ref[0:96, 0:128], jnp.concatenate(halves(plane_weight * right), 0)
    )
    start_each(lambda copy: copy.start(), 1)
    loads[2].wait()
    class_ref[0:1, 0:16] = element_ref[...].astype(F32)
    deep_start(1)
    deep_start(2)
    for load in loads[3:]:
        load.wait()

    blank = jnp.zeros((6, 32), F32)
    groups = (
        [vectors_ref[a, :, 0, :] for a in range(10)]
        + [vectors_ref[b, :, 1, :] for b in range(10)]
        + [vectors_ref[:, n, 1, :] for n in range(10)]
        + [vectors_ref[:, p, 2, :] for p in range(10)]
        + [values_ref[:, d, :] for d in (1, 0, 2)]
    )
    entries = jnp.concatenate([part for group in groups for part in (group, blank)], 0)
    corner = lax.broadcasted_iota(jnp.int32, (256, 256), 0) // 8
    along = lax.broadcasted_iota(jnp.int32, (256, 256), 1) // 8
    high, low = halves(jnp.where(corner == along, jnp.concatenate([deep_ref[...]] * 32, 0), 0.0))
    deep_high[...] = high
    deep_low[...] = low
    deep_wait(1)

    def element_of(shape):
        place_at = lax.rem(lax.broadcasted_iota(jnp.int32, shape, 1), 24)
        return jnp.where(place_at < 20, place_at, place_at - 24)

    source = lax.broadcasted_iota(jnp.int32, (384, 256), 0)
    source = jnp.where(source < 128, source, jnp.where(source < 256, source - 112, source - 272))
    known = jnp.concatenate([class_ref[...], class_recv[1], class_recv[0]], 1).astype(BF16)
    classes = jnp.dot(
        known,
        (source == element_of((384, 256))).astype(F32).astype(BF16),
        preferred_element_type=F32,
    )[0:1]
    kind = lax.broadcasted_iota(jnp.int32, (32, 256), 0).astype(F32)
    chooser = (jnp.abs(kind - classes) < 0.5).astype(F32).astype(BF16)
    table = place(entries, chooser, plain)
    for a in range(10):
        for m in range(10):
            first_ref[a, m] = jnp.broadcast_to(table[a * 16 + m : a * 16 + m + 1], (16, 256))
    second_ref[...] = table[160:320].reshape(10, 16, 256)
    second_back_ref[...] = table[320:480].reshape(10, 16, 256)
    mode = lax.broadcasted_iota(jnp.int32, (1, 256), 1) // 24
    third = jnp.zeros((16, 256), F32)
    level = jnp.zeros((1, 256), F32)
    for p in range(10):
        third = third + jnp.where(mode == p, table[480 + 16 * p : 496 + 16 * p], 0.0)
        level = level + jnp.where(mode == p, table[672 + p : 673 + p], 0.0)

    for m in range(10):
        inverse_ref[m] = 1.0 / (table[656 + m : 657 + m] + table[640:656] + level)
    node = lax.broadcasted_iota(jnp.int32, (256, 256), 0)
    node = jnp.where(node < 192, node, node - 256)
    element = element_of((256, 256))
    reach = node - 8 * element
    slot = jnp.where(
        reach == -2, 0, jnp.where(reach == 9, 9, jnp.where((reach >= 0) & (reach < 8), reach + 1, -1))
    )
    slot_back = jnp.where(reach == 8, 8, jnp.where(reach == -1, 1, slot))
    inside = (
        (16 * gz + element >= 0)
        & (16 * gz + element < 16 * nz)
        & (128 * gz + node >= 0)
        & (128 * gz + node < 128 * nz)
    )
    slot = jnp.where(inside, slot, -1)
    slot_back = jnp.where(inside, slot_back, -1)
    spread = jnp.zeros((256, 256), F32)
    spread_back = jnp.zeros((256, 256), F32)
    for c in range(10):
        spread = jnp.where(slot == c, third[c : c + 1], spread)
        spread_back = jnp.where(slot_back == c, third[c : c + 1], spread_back)
    third_high[...], third_low[...] = halves(spread)
    back_high[...], back_low[...] = halves(spread_back)

    deep_wait(0)
    start_each(lambda copy: copy.wait_recv(), -1)
    wide = jnp.concatenate([plane_weight, plane_weight], 1) * widen(right, right_recv[...])
    extended = gather_plane_end(
        wide, widen(start_recv[0], (start_recv[1], start_recv[2]))
    )
    wide_precond = scatter(1, solve(extended))
    deep_wait(2)
    wide_geometry[...] = widen(geometry_ref[...], geometry_recv[...])
    image_local = local(wide_precond, *slopes_of(wide_precond))
    wide = sum_deep(image_local)
    gather_plane_start(2, wide)
    extended = gather_plane_end(wide, plane_wait(2))
    image = jnp.concatenate(
        [extended[16 * x + 1 : 16 * x + 9, 0:128] for x in range(1, 9)], 0
    )
    wide_again = scatter(3, solve(extended))
    slopes, deep = slopes_of(wide_again)
    precond, again = wide_precond[:, 0:128], wide_again[:, 0:128]

    own = geometry_ref[...]
    energy = (
        own[0:64] * slopes[0:64, 0:128] * slopes[0:64, 0:128]
        + own[64:128] * slopes[64:128, 0:128] * slopes[64:128, 0:128]
        + own[128:192] * deep[:, 0:128] * deep[:, 0:128]
        + own[192:256] * again * again
    )
    products = (
        weighted * precond,
        precond * image_local[:, 0:128],
        weighted * again,
        weight * image * again,
        energy,
    )
    kind = lax.broadcasted_iota(jnp.int32, (8, 128), 0)
    packed = jnp.zeros((8, 128), F32)
    for number, entry in enumerate(products):
        packed = packed + jnp.where(kind == number, jnp.sum(entry, 0, keepdims=True), 0.0)

    def sum_copy(buffer, send_sems, recv_sems, offset, mine, partner):
        return pltpu.make_async_remote_copy(
            src_ref=buffer.at[mine],
            dst_ref=buffer.at[mine],
            send_sem=send_sems.at[offset - 1],
            recv_sem=recv_sems.at[mine],
            device_id=partner,
            device_id_type=MESH,
        )

    def sum_wait(buffer, recv_sems, other):
        pltpu.make_async_copy(buffer.at[other], buffer.at[other], recv_sems.at[other]).wait()

    sums_plane[me_plane] = packed
    for offset in range(1, plane_size):
        sum_copy(
            sums_plane, sum_send_sems, sum_plane_sems, offset, me_plane, plane_partner(offset)[1]
        ).start()
    wide = sum_deep(local(wide_again, slopes, deep))
    gather_plane_start(4, wide)
    for offset in range(1, plane_size):
        sum_wait(sums_plane, sum_plane_sems, plane_partner(offset)[0])
    sums_line[gz] = jnp.sum(sums_plane[...], 0)
    for offset in range(1, nz):
        sum_copy(
            sums_line, line_send_sems, sum_line_sems, offset, gz, line_partner(offset)[1]
        ).start()
    extended = gather_plane_end(wide, plane_wait(4))
    again_image = jnp.concatenate(
        [extended[16 * x + 1 : 16 * x + 9, 0:128] for x in range(1, 9)], 0
    )
    for offset in range(1, nz):
        sum_wait(sums_line, sum_line_sems, line_partner(offset)[0])
    sums = jnp.sum(jnp.sum(sums_line[...], 0), 1, keepdims=True)
    a, b, c, d, f = [sums[k : k + 1] for k in range(5)]
    step_one = a / b
    rho = a - step_one * (b + c) + step_one * step_one * d
    stretch = 1.0 + rho / a
    curvature = stretch * stretch * b - 2.0 * stretch * step_one * d + step_one * step_one * f
    step_two = rho / curvature
    on_precond = step_one + step_two * stretch
    on_again = step_one * step_two
    result_ref[0] = on_precond * precond - on_again * again
    result_ref[1] = right - on_precond * image + on_again * again_image

    for number in range(3):
        for step in (1, -1):
            pl.when(deep_exists(step))(
                lambda number=number, step=step: deep_copy(number, step).wait_send()
            )
    start_each(lambda copy: copy.wait_send(), 1)
    for number in range(1, ROUNDS):
        for at, (dx, dy) in enumerate(DIRECTIONS):
            pl.when(plane_exists(dx, dy))(
                lambda number=number, at=at: plane_copy(number, at).wait_send()
            )
    for offset in range(1, plane_size):
        sum_copy(
            sums_plane, sum_send_sems, sum_plane_sems, offset, me_plane, plane_partner(offset)[1]
        ).wait_send()
    for offset in range(1, nz):
        sum_copy(
            sums_line, line_send_sems, sum_line_sems, offset, gz, line_partner(offset)[1]
        ).wait_send()


def on_device(counts, right_side, geometry, element_shape_class, fdm_vectors, fdm_values):
    nx, ny, nz = counts
    shape = right_side.shape
    vmem = pl.BlockSpec(memory_space=pltpu.VMEM)
    result = pl.pallas_call(
        lambda *refs: kernel(counts, *refs),
        out_shape=jax.ShapeDtypeStruct((2, 64, 128), F32),
        in_specs=[pl.BlockSpec(memory_space=pl.ANY)] * 7,
        out_specs=vmem,
        scratch_shapes=[
            pltpu.VMEM((64, 128), F32),
            pltpu.VMEM((256, 128), F32),
            pltpu.VMEM((1, 16), jnp.int32),
            pltpu.VMEM((10, 10, 3, 32), F32),
            pltpu.VMEM((10, 3, 32), F32),
            pltpu.VMEM((608, 256), BF16),
            pltpu.VMEM((8, 256), F32),
            pltpu.VMEM((96, 128), F32),
            pltpu.VMEM((3, 96, 128), F32),
            pltpu.VMEM((2, 64, 128), F32),
            pltpu.VMEM((2, 256, 128), F32),
            pltpu.VMEM((2, 8, 128), F32),
            pltpu.VMEM((256, 256), F32),
            pltpu.VMEM((8, 128), F32),
            pltpu.VMEM((256, 256), BF16),
            pltpu.VMEM((256, 256), BF16),
            pltpu.VMEM((ROUNDS, 96, 256), F32),
            pltpu.VMEM((ROUNDS, 96, 256), F32),
            pltpu.VMEM((10, 10, 16, 256), F32),
            pltpu.VMEM((10, 16, 256), F32),
            pltpu.VMEM((10, 16, 256), F32),
            pltpu.VMEM((256, 256), BF16),
            pltpu.VMEM((256, 256), BF16),
            pltpu.VMEM((256, 256), BF16),
            pltpu.VMEM((256, 256), BF16),
            pltpu.VMEM((10, 16, 256), F32),
            pltpu.VMEM((nx * ny, 8, 128), F32),
            pltpu.VMEM((nz, 8, 128), F32),
            pltpu.SemaphoreType.DMA((7,)),
            pltpu.SemaphoreType.DMA((2, 3, 8)),
            pltpu.SemaphoreType.DMA((2, 3, 2)),
            pltpu.SemaphoreType.DMA((2, ROUNDS, 8)),
            pltpu.SemaphoreType.DMA((nx * ny,)),
            pltpu.SemaphoreType.DMA((nx * ny,)),
            pltpu.SemaphoreType.DMA((nz,)),
            pltpu.SemaphoreType.DMA((nz,)),
        ],
        compiler_params=pltpu.CompilerParams(
            collective_id=0, has_side_effects=True, vmem_limit_bytes=60 * 1024 * 1024
        ),
    )(
        right_side.reshape(64, 128),
        geometry.reshape(256, 128),
        element_shape_class.reshape(1, 16),
        jnp.transpose(fdm_vectors, (2, 3, 1, 0)),
        jnp.transpose(fdm_values, (2, 1, 0)),
        jnp.asarray(selections(), BF16),
        jnp.asarray(np.tile(derivative_table().T, (1, 32)), F32),
    )
    return result[0].reshape(shape), result[1].reshape(shape)


def solution(mesh):
    counts = tuple(mesh.shape[name] for name in ("gx", "gy", "gz"))
    placed = (P("gx", "gy", "gz"), P(None, "gx", "gy", "gz"), P("gx", "gy", "gz"), P(), P())
    return jax.shard_map(
        lambda *arrays: on_device(counts, *arrays),
        mesh=mesh,
        in_specs=placed,
        out_specs=(P("gx", "gy", "gz"), P("gx", "gy", "gz")),
        check_vma=False,
    )
```

```python
import jax
import jax.numpy as jnp
import numpy as np
from jax import lax
from jax.experimental import pallas as pl
from jax.experimental.pallas import tpu as pltpu
from jax.sharding import PartitionSpec as P

MESH = pl.DeviceIdType.MESH
F32 = jnp.float32
BF16 = jnp.bfloat16
DIRECTIONS = ((1, 0), (-1, 0), (0, 1), (0, -1), (1, 1), (1, -1), (-1, 1), (-1, -1))
STARTS = (0, 16, 32, 48, 64, 72, 80, 88, 96)
ROUNDS = 5
LEVELS = (0, 1, -1)


def derivative_table():
    points = np.array(
        [
            -1.0,
            -0.8717401485096066,
            -0.5917001814331423,
            -0.2092992179024789,
            0.2092992179024789,
            0.5917001814331423,
            0.8717401485096066,
            1.0,
        ]
    )
    previous = np.ones(8)
    current = points * 1.0
    for order in range(1, 7):
        following = ((2 * order + 1) * points * current - order * previous) / (order + 1)
        previous = current
        current = following
    spacing = points[:, None] - points[None, :] + np.eye(8)
    off_diagonal = current[:, None] / (current[None, :] * spacing)
    positions = np.arange(8)
    end_values = np.where(positions == 0, -14.0, 0.0) + np.where(positions == 7, 14.0, 0.0)
    return np.where(np.eye(8) > 0, np.eye(8) * end_values[None, :], off_diagonal)


def message_rows(sent):
    own = tuple(range(1, 9))
    for place, (dx, dy) in enumerate(DIRECTIONS):
        xs = sent[dx] if dx else own
        ys = sent[dy] if dy else own
        if dy and not dx:
            pairs = [(x, y) for y in ys for x in xs]
        else:
            pairs = [(x, y) for x in xs for y in ys]
        for number, (x, y) in enumerate(pairs):
            yield STARTS[place] + number, x, y


def node_row(x, y):
    return (x - 1) * 8 + y - 1


def slot_row(x, y):
    return x * 16 + y


def selections():
    gather_from = {1: (7, 8), -1: (2, 1)}
    gather_to = {1: (0, 1), -1: (9, 8)}
    scatter_from = {1: (9, 8), -1: (0, 1)}
    scatter_to = {1: (2, 1), -1: (7, 8)}
    pack_gather = np.zeros((96, 128))
    unpack_gather = np.zeros((160, 160))
    pack_scatter = np.zeros((96, 160))
    unpack_scatter = np.zeros((64, 256))
    for x in range(1, 9):
        for y in range(1, 9):
            unpack_gather[slot_row(x, y), node_row(x, y)] = 1
            unpack_scatter[node_row(x, y), slot_row(x, y)] = 1
    for row, x, y in message_rows(gather_from):
        pack_gather[row, [node_row(x, y), 64 + node_row(x, y)]] = 1
    for row, x, y in message_rows(gather_to):
        unpack_gather[slot_row(x, y), 64 + row] = 1
    for row, x, y in message_rows(scatter_from):
        pack_scatter[row, slot_row(x, y)] = 1
    for row, x, y in message_rows(scatter_to):
        unpack_scatter[node_row(x, y), 160 + row] = 1
    derivative = derivative_table()
    eye = np.eye(8)
    plane = np.concatenate([np.kron(derivative, eye), np.kron(eye, derivative)], 0)
    high = np.asarray(np.asarray(plane, BF16), np.float64)
    low = plane - high
    table = np.zeros((608, 256))
    for start, part in (
        (0, pack_gather),
        (96, unpack_gather),
        (256, pack_scatter),
        (352, unpack_scatter),
        (416, np.concatenate([high, high, low], 1)),
        (544, np.concatenate([high.T, low.T], 1)),
    ):
        table[start : start + part.shape[0], : part.shape[1]] = part
    return table


def halves(value):
    high = value.astype(BF16)
    return high, (value - high.astype(F32)).astype(BF16)


def product(left, right, dims=((1,), (0,))):
    return lax.dot_general(left, right, (dims, ((), ())), preferred_element_type=F32)


def pick(chooser, value):
    high, low = halves(value)
    return product(chooser, low) + product(chooser, high)


def times(value, high_ref, low_ref, dims=((1,), (0,))):
    high, low = halves(value)
    return (
        product(low, high_ref[...], dims)
        + product(high, low_ref[...], dims)
        + product(high, high_ref[...], dims)
    )


def place(value, chooser, dims):
    total = None
    for piece in pieces(value):
        part = lax.dot_general(piece, chooser, (dims, ((), ())), preferred_element_type=F32)
        total = part if total is None else total + part
    return total


def kernel(
    counts,
    right_hbm,
    geometry_hbm,
    element_hbm,
    vectors_hbm,
    values_hbm,
    select_hbm,
    deep_hbm,
    result_ref,
    right_ref,
    geometry_ref,
    element_ref,
    vectors_ref,
    values_ref,
    select_ref,
    deep_ref,
    start_send,
    start_recv,
    right_recv,
    geometry_recv,
    class_recv,
    wide_geometry,
    class_ref,
    entries_ref,
    own_ref,
    beside_ref,
    deep_high,
    deep_low,
    plane_send,
    plane_recv,
    first_ref,
    second_ref,
    second_back_ref,
    third_high,
    third_low,
    back_high,
    back_low,
    inverse_ref,
    sums_plane,
    sums_line,
    load_sems,
    start_sems,
    deep_sems,
    plane_sems,
    sum_send_sems,
    sum_plane_sems,
    line_send_sems,
    sum_line_sems,
):
    nx, ny, nz = counts
    gx, gy, gz = lax.axis_index("gx"), lax.axis_index("gy"), lax.axis_index("gz")
    plane_size = nx * ny
    me_plane = gx * ny + gy

    loads = [
        pltpu.make_async_copy(source, target, load_sems.at[number])
        for number, (source, target) in enumerate(
            (
                (right_hbm, right_ref),
                (select_hbm, select_ref),
                (element_hbm, element_ref),
                (vectors_hbm, vectors_ref),
                (values_hbm, values_ref),
                (deep_hbm, deep_ref),
                (geometry_hbm, geometry_ref),
            )
        )
    ]
    for load in loads:
        load.start()

    start_recv[...] = jnp.zeros_like(start_recv)
    right_recv[...] = jnp.zeros_like(right_recv)
    geometry_recv[...] = jnp.zeros_like(geometry_recv)
    class_recv[...] = jnp.zeros_like(class_recv)
    plane_recv[...] = jnp.zeros_like(plane_recv)

    def plane_partner(offset):
        other = lax.rem(me_plane + offset, plane_size)
        return other, (other // ny, lax.rem(other, ny), gz)

    def line_partner(offset):
        other = lax.rem(gz + offset, nz)
        return other, (gx, gy, other)

    class_ref[...] = jnp.zeros_like(class_ref)

    def exists(dx, dy, dz):
        x, y, z = gx + dx, gy + dy, gz + dz
        return (x >= 0) & (x < nx) & (y >= 0) & (y < ny) & (z >= 0) & (z < nz)

    barrier = pltpu.get_barrier_semaphore()
    for offset in range(1, plane_size):
        pl.semaphore_signal(
            barrier, inc=1, device_id=plane_partner(offset)[1], device_id_type=MESH
        )
    for offset in range(1, nz):
        pl.semaphore_signal(barrier, inc=1, device_id=line_partner(offset)[1], device_id_type=MESH)
    slanted = [(dx, dy, dz) for dz in (1, -1) for dx, dy in DIRECTIONS]
    partners = plane_size + nz - 2
    for step in slanted:
        pl.when(exists(*step))(
            lambda step=step: pl.semaphore_signal(
                barrier,
                inc=1,
                device_id=(gx + step[0], gy + step[1], gz + step[2]),
                device_id_type=MESH,
            )
        )
        partners = partners + exists(*step).astype(jnp.int32)
    pl.semaphore_wait(barrier, partners)

    inputs = (
        (right_hbm, right_recv),
        (class_ref, class_recv),
        (geometry_hbm, geometry_recv),
    )

    def deep_copy(number, step):
        side = 0 if step > 0 else 1
        mine, theirs = inputs[number]
        return pltpu.make_async_remote_copy(
            src_ref=mine,
            dst_ref=theirs.at[side],
            send_sem=deep_sems.at[0, number, side],
            recv_sem=deep_sems.at[1, number, side],
            device_id=(gx, gy, gz + step),
            device_id_type=MESH,
        )

    def deep_exists(step):
        return gz + 1 < nz if step > 0 else gz > 0

    def deep_start(number):
        for step in (1, -1):
            pl.when(deep_exists(step))(lambda step=step: deep_copy(number, step).start())

    def deep_wait(number):
        for step in (1, -1):
            pl.when(deep_exists(-step))(lambda step=step: deep_copy(number, step).wait_recv())

    def widen(own, received):
        half = lax.broadcasted_iota(jnp.int32, own.shape, 1) < 64
        return jnp.concatenate([own, jnp.where(half, received[1], received[0])], 1)

    def plane_copy(number, at):
        dx, dy = DIRECTIONS[at]
        rows = pl.ds(STARTS[at], STARTS[at + 1] - STARTS[at])
        return pltpu.make_async_remote_copy(
            src_ref=plane_send.at[number, rows],
            dst_ref=plane_recv.at[number, rows],
            send_sem=plane_sems.at[0, number, at],
            recv_sem=plane_sems.at[1, number, at],
            device_id=(gx + dx, gy + dy, gz),
            device_id_type=MESH,
        )

    def plane_exists(dx, dy):
        return exists(dx, dy, 0)

    def start_copy(level, at):
        dx, dy = DIRECTIONS[at]
        rows = pl.ds(STARTS[at], STARTS[at + 1] - STARTS[at])
        return pltpu.make_async_remote_copy(
            src_ref=start_send.at[rows],
            dst_ref=start_recv.at[level, rows],
            send_sem=start_sems.at[0, level, at],
            recv_sem=start_sems.at[1, level, at],
            device_id=(gx + dx, gy + dy, gz + LEVELS[level]),
            device_id_type=MESH,
        )

    def start_each(action, sign):
        for level, dz in enumerate(LEVELS):
            for at, (dx, dy) in enumerate(DIRECTIONS):
                pl.when(exists(sign * dx, sign * dy, sign * dz))(
                    lambda level=level, at=at: action(start_copy(level, at))
                )

    def plane_start(number, message):
        plane_send[number] = message
        for at, (dx, dy) in enumerate(DIRECTIONS):
            pl.when(plane_exists(dx, dy))(lambda at=at: plane_copy(number, at).start())

    def plane_wait(number):
        for at, (dx, dy) in enumerate(DIRECTIONS):
            pl.when(plane_exists(-dx, -dy))(lambda at=at: plane_copy(number, at).wait_recv())
        return plane_recv[number]

    rows = lax.broadcasted_iota(jnp.int32, (64, 128), 0)
    lanes = lax.broadcasted_iota(jnp.int32, (64, 128), 1)
    plain = ((1,), (0,))
    rows_rows = ((1,), (1,))

    def sum_deep(field):
        node = lax.rem(lax.broadcasted_iota(jnp.int32, (64, 256), 1), 8)
        following = jnp.where(node == 7, pltpu.roll(field, 255, 1), 0.0)
        previous = jnp.where(node == 0, pltpu.roll(field, 1, 1), 0.0)
        return field + following + previous

    def gather_plane_start(number, wide):
        plane_start(number, product(select_ref[0:96, 0:128], jnp.concatenate(halves(wide), 0)))

    def gather_plane_end(wide, received):
        both = jnp.concatenate([wide, received], 0)
        return pick(select_ref[96:256, 0:160], both)

    def scatter(number, extended):
        plane_start(number, pick(select_ref[256:352, 0:160], extended))
        both = jnp.concatenate([extended, plane_wait(number)], 0)
        return pick(select_ref[352:416, :], both)

    def solve(extended):
        value = times(extended, third_high, third_low).reshape(10, 16, 256)
        value = value.reshape(10, 1, 2, 8, 256)
        total = first_ref[0][:, None] * value[0]
        for a in range(1, 10):
            total = total + first_ref[a][:, None] * value[a]
        value = total.reshape(10, 16, 256)
        total = second_ref[0][None] * value[:, 0:1, :]
        for b in range(1, 10):
            total = total + second_ref[b][None] * value[:, b : b + 1, :]
        value = total * inverse_ref[...]
        total = second_back_ref[0][None] * value[:, 0:1, :]
        for n in range(1, 10):
            total = total + second_back_ref[n][None] * value[:, n : n + 1, :]
        value = total.reshape(10, 1, 2, 8, 256)
        total = first_ref[:, 0][:, None] * value[0]
        for m in range(1, 10):
            total = total + first_ref[:, m][:, None] * value[m]
        return times(total.reshape(160, 256), back_high, back_low, rows_rows)

    def slopes_of(field):
        high, low = halves(field)
        slopes = product(select_ref[416:544, 0:192], jnp.concatenate([high, low, high], 0))
        return slopes, times(field, deep_high, deep_low)

    def local(field, slopes, deep):
        high, low = halves(wide_geometry[0:128] * slopes)
        back = (
            product(select_ref[544:608, 0:128], low)
            + product(select_ref[544:608, 128:256], high)
            + product(select_ref[544:608, 0:128], high)
        )
        deep = times(wide_geometry[128:192] * deep, deep_high, deep_low, rows_rows)
        return back + deep + wide_geometry[192:256] * field

    def factor(inside, length, device, devices):
        last = (device == devices - 1) & (inside == length - 1)
        first = (device == 0) & (inside == 0)
        node = lax.rem(inside, 8)
        shared = ((node == 7) & ~last) | ((node == 0) & ~first)
        return jnp.where(shared, 0.5, 1.0).astype(F32)

    plane_weight = factor(rows // 8, 8, gx, nx) * factor(lax.rem(rows, 8), 8, gy, ny)
    weight = plane_weight * factor(lanes, 128, gz, nz)
    deep_start(0)
    loads[0].wait()
    loads[1].wait()
    right = right_ref[...]
    weighted = weight * right
    start_send[...] = product(
        select_ref[0:96, 0:128], jnp.concatenate(halves(plane_weight * right), 0)
    )
    start_each(lambda copy: copy.start(), 1)
    loads[2].wait()
    class_ref[0:1, 0:16] = element_ref[...].astype(F32)
    deep_start(1)
    deep_start(2)
    for load in loads[3:]:
        load.wait()

    blank = jnp.zeros((6, 32), F32)
    groups = (
        [vectors_ref[a, :, 0, :] for a in range(10)]
        + [vectors_ref[b, :, 1, :] for b in range(10)]
        + [vectors_ref[:, n, 1, :] for n in range(10)]
        + [vectors_ref[:, p, 2, :] for p in range(10)]
        + [values_ref[:, d, :] for d in (1, 0, 2)]
    )
    entries = jnp.concatenate([part for group in groups for part in (group, blank)], 0)
    entries_ref[...] = jnp.concatenate(halves(entries), 1)
    corner = lax.broadcasted_iota(jnp.int32, (256, 256), 0) // 8
    along = lax.broadcasted_iota(jnp.int32, (256, 256), 1) // 8
    high, low = halves(jnp.where(corner == along, jnp.concatenate([deep_ref[...]] * 32, 0), 0.0))
    deep_high[...] = high
    deep_low[...] = low
    def element_of(shape):
        place_at = lax.rem(lax.broadcasted_iota(jnp.int32, shape, 1), 24)
        return jnp.where(place_at < 20, place_at, place_at - 24)

    node = lax.broadcasted_iota(jnp.int32, (256, 256), 0)
    node = jnp.where(node < 192, node, node - 256)
    element = element_of((256, 256))
    reach = node - 8 * element
    inside = (
        (16 * gz + element >= 0)
        & (16 * gz + element < 16 * nz)
        & (128 * gz + node >= 0)
        & (128 * gz + node < 128 * nz)
    )
    beside = (reach == -2) | (reach == -1) | (reach == 8) | (reach == 9)
    own_ref[...] = jnp.where(inside & (reach >= 0) & (reach < 8), 1.0, 0.0)
    beside_ref[...] = jnp.where(inside & beside, 1.0, 0.0)
    deep_wait(1)

    source = lax.broadcasted_iota(jnp.int32, (384, 256), 0)
    source = jnp.where(source < 128, source, jnp.where(source < 256, source - 112, source - 272))
    known = jnp.concatenate([class_ref[...], class_recv[1], class_recv[0]], 1).astype(BF16)
    classes = jnp.dot(
        known,
        (source == element_of((384, 256))).astype(F32).astype(BF16),
        preferred_element_type=F32,
    )[0:1]
    kind = lax.rem(lax.broadcasted_iota(jnp.int32, (64, 256), 0), 32).astype(F32)
    chooser = (jnp.abs(kind - classes) < 0.5).astype(F32).astype(BF16)
    table = product(entries_ref[...], chooser)
    for a in range(10):
        for m in range(10):
            first_ref[a, m] = jnp.broadcast_to(table[a * 16 + m : a * 16 + m + 1], (8, 256))
    second_ref[...] = table[160:320].reshape(10, 16, 256)
    second_back_ref[...] = table[320:480].reshape(10, 16, 256)
    mode = lax.broadcasted_iota(jnp.int32, (1, 256), 1) // 24
    third = jnp.zeros((16, 256), F32)
    level = jnp.zeros((1, 256), F32)
    for p in range(10):
        third = third + jnp.where(mode == p, table[480 + 16 * p : 496 + 16 * p], 0.0)
        level = level + jnp.where(mode == p, table[672 + p : 673 + p], 0.0)

    for m in range(10):
        inverse_ref[m] = 1.0 / (table[656 + m : 657 + m] + table[640:656] + level)
    ends = [third[c : c + 1] for c in (8, 9, 0, 1)]
    none = jnp.zeros((4, 256), F32)
    inner = third[1:9]
    reached = jnp.concatenate([none[0:1], ends[1], none, ends[2], none[0:1]], 0)
    shared = jnp.concatenate([ends[0], ends[1], none, ends[2], ends[3]], 0)
    for outer, high_ref, low_ref in (
        (reached, third_high, third_low),
        (shared, back_high, back_low),
    ):
        for group in range(16):
            at = pl.ds(16 * group, 16)
            spread = own_ref[at] * jnp.concatenate([inner] * 2, 0) + beside_ref[
                at
            ] * jnp.concatenate([outer] * 2, 0)
            high_ref[at], low_ref[at] = halves(spread)

    deep_wait(0)
    start_each(lambda copy: copy.wait_recv(), -1)
    wide = jnp.concatenate([plane_weight, plane_weight], 1) * widen(right, right_recv[...])
    extended = gather_plane_end(
        wide, widen(start_recv[0], (start_recv[1], start_recv[2]))
    )
    wide_precond = scatter(1, solve(extended))
    deep_wait(2)
    wide_geometry[...] = widen(geometry_ref[...], geometry_recv[...])
    image_local = local(wide_precond, *slopes_of(wide_precond))
    wide = sum_deep(image_local)
    gather_plane_start(2, wide)
    extended = gather_plane_end(wide, plane_wait(2))
    image = jnp.concatenate(
        [extended[16 * x + 1 : 16 * x + 9, 0:128] for x in range(1, 9)], 0
    )
    wide_again = scatter(3, solve(extended))
    slopes, deep = slopes_of(wide_again)
    precond, again = wide_precond[:, 0:128], wide_again[:, 0:128]

    own = geometry_ref[...]
    energy = (
        own[0:64] * slopes[0:64, 0:128] * slopes[0:64, 0:128]
        + own[64:128] * slopes[64:128, 0:128] * slopes[64:128, 0:128]
        + own[128:192] * deep[:, 0:128] * deep[:, 0:128]
        + own[192:256] * again * again
    )
    products = (
        weighted * precond,
        precond * image_local[:, 0:128],
        weighted * again,
        weight * image * again,
        energy,
    )
    kind = lax.broadcasted_iota(jnp.int32, (8, 128), 0)
    packed = jnp.zeros((8, 128), F32)
    for number, entry in enumerate(products):
        packed = packed + jnp.where(kind == number, jnp.sum(entry, 0, keepdims=True), 0.0)

    def sum_copy(buffer, send_sems, recv_sems, offset, mine, partner):
        return pltpu.make_async_remote_copy(
            src_ref=buffer.at[mine],
            dst_ref=buffer.at[mine],
            send_sem=send_sems.at[offset - 1],
            recv_sem=recv_sems.at[mine],
            device_id=partner,
            device_id_type=MESH,
        )

    def sum_wait(buffer, recv_sems, other):
        pltpu.make_async_copy(buffer.at[other], buffer.at[other], recv_sems.at[other]).wait()

    sums_plane[me_plane] = packed
    for offset in range(1, plane_size):
        sum_copy(
            sums_plane, sum_send_sems, sum_plane_sems, offset, me_plane, plane_partner(offset)[1]
        ).start()
    wide = sum_deep(local(wide_again, slopes, deep))
    gather_plane_start(4, wide)
    for offset in range(1, plane_size):
        sum_wait(sums_plane, sum_plane_sems, plane_partner(offset)[0])
    sums_line[gz] = jnp.sum(sums_plane[...], 0)
    for offset in range(1, nz):
        sum_copy(
            sums_line, line_send_sems, sum_line_sems, offset, gz, line_partner(offset)[1]
        ).start()
    extended = gather_plane_end(wide, plane_wait(4))
    again_image = jnp.concatenate(
        [extended[16 * x + 1 : 16 * x + 9, 0:128] for x in range(1, 9)], 0
    )
    for offset in range(1, nz):
        sum_wait(sums_line, sum_line_sems, line_partner(offset)[0])
    sums = jnp.sum(jnp.sum(sums_line[...], 0), 1, keepdims=True)
    a, b, c, d, f = [sums[k : k + 1] for k in range(5)]
    step_one = a / b
    rho = a - step_one * (b + c) + step_one * step_one * d
    stretch = 1.0 + rho / a
    curvature = stretch * stretch * b - 2.0 * stretch * step_one * d + step_one * step_one * f
    step_two = rho / curvature
    on_precond = step_one + step_two * stretch
    on_again = step_one * step_two
    result_ref[0] = on_precond * precond - on_again * again
    result_ref[1] = right - on_precond * image + on_again * again_image

    for number in range(3):
        for step in (1, -1):
            pl.when(deep_exists(step))(
                lambda number=number, step=step: deep_copy(number, step).wait_send()
            )
    start_each(lambda copy: copy.wait_send(), 1)
    for number in range(1, ROUNDS):
        for at, (dx, dy) in enumerate(DIRECTIONS):
            pl.when(plane_exists(dx, dy))(
                lambda number=number, at=at: plane_copy(number, at).wait_send()
            )
    for offset in range(1, plane_size):
        sum_copy(
            sums_plane, sum_send_sems, sum_plane_sems, offset, me_plane, plane_partner(offset)[1]
        ).wait_send()
    for offset in range(1, nz):
        sum_copy(
            sums_line, line_send_sems, sum_line_sems, offset, gz, line_partner(offset)[1]
        ).wait_send()


def on_device(counts, right_side, geometry, element_shape_class, fdm_vectors, fdm_values):
    nx, ny, nz = counts
    shape = right_side.shape
    vmem = pl.BlockSpec(memory_space=pltpu.VMEM)
    result = pl.pallas_call(
        lambda *refs: kernel(counts, *refs),
        out_shape=jax.ShapeDtypeStruct((2, 64, 128), F32),
        in_specs=[pl.BlockSpec(memory_space=pl.ANY)] * 7,
        out_specs=vmem,
        scratch_shapes=[
            pltpu.VMEM((64, 128), F32),
            pltpu.VMEM((256, 128), F32),
            pltpu.VMEM((1, 16), jnp.int32),
            pltpu.VMEM((10, 10, 3, 32), F32),
            pltpu.VMEM((10, 3, 32), F32),
            pltpu.VMEM((608, 256), BF16),
            pltpu.VMEM((8, 256), F32),
            pltpu.VMEM((96, 128), F32),
            pltpu.VMEM((3, 96, 128), F32),
            pltpu.VMEM((2, 64, 128), F32),
            pltpu.VMEM((2, 256, 128), F32),
            pltpu.VMEM((2, 8, 128), F32),
            pltpu.VMEM((256, 256), F32),
            pltpu.VMEM((8, 128), F32),
            pltpu.VMEM((688, 64), BF16),
            pltpu.VMEM((256, 256), F32),
            pltpu.VMEM((256, 256), F32),
            pltpu.VMEM((256, 256), BF16),
            pltpu.VMEM((256, 256), BF16),
            pltpu.VMEM((ROUNDS, 96, 256), F32),
            pltpu.VMEM((ROUNDS, 96, 256), F32),
            pltpu.VMEM((10, 10, 8, 256), F32),
            pltpu.VMEM((10, 16, 256), F32),
            pltpu.VMEM((10, 16, 256), F32),
            pltpu.VMEM((256, 256), BF16),
            pltpu.VMEM((256, 256), BF16),
            pltpu.VMEM((256, 256), BF16),
            pltpu.VMEM((256, 256), BF16),
            pltpu.VMEM((10, 16, 256), F32),
            pltpu.VMEM((nx * ny, 8, 128), F32),
            pltpu.VMEM((nz, 8, 128), F32),
            pltpu.SemaphoreType.DMA((7,)),
            pltpu.SemaphoreType.DMA((2, 3, 8)),
            pltpu.SemaphoreType.DMA((2, 3, 2)),
            pltpu.SemaphoreType.DMA((2, ROUNDS, 8)),
            pltpu.SemaphoreType.DMA((nx * ny,)),
            pltpu.SemaphoreType.DMA((nx * ny,)),
            pltpu.SemaphoreType.DMA((nz,)),
            pltpu.SemaphoreType.DMA((nz,)),
        ],
        compiler_params=pltpu.CompilerParams(
            collective_id=0, has_side_effects=True, vmem_limit_bytes=60 * 1024 * 1024
        ),
    )(
        right_side.reshape(64, 128),
        geometry.reshape(256, 128),
        element_shape_class.reshape(1, 16),
        jnp.transpose(fdm_vectors, (2, 3, 1, 0)),
        jnp.transpose(fdm_values, (2, 1, 0)),
        jnp.asarray(selections(), BF16),
        jnp.asarray(np.tile(derivative_table().T, (1, 32)), F32),
    )
    return result[0].reshape(shape), result[1].reshape(shape)


def solution(mesh):
    counts = tuple(mesh.shape[name] for name in ("gx", "gy", "gz"))
    placed = (P("gx", "gy", "gz"), P(None, "gx", "gy", "gz"), P("gx", "gy", "gz"), P(), P())
    return jax.shard_map(
        lambda *arrays: on_device(counts, *arrays),
        mesh=mesh,
        in_specs=placed,
        out_specs=(P("gx", "gy", "gz"), P("gx", "gy", "gz")),
        check_vma=False,
    )
```

```python
import jax
import jax.numpy as jnp
import numpy as np
from jax import lax
from jax.experimental import pallas as pl
from jax.experimental.pallas import tpu as pltpu
from jax.sharding import PartitionSpec as P

MESH = pl.DeviceIdType.MESH
F32 = jnp.float32
BF16 = jnp.bfloat16
DIRECTIONS = ((1, 0), (-1, 0), (0, 1), (0, -1), (1, 1), (1, -1), (-1, 1), (-1, -1))
STARTS = (0, 16, 32, 48, 64, 72, 80, 88, 96)
ROUNDS = 5
LEVELS = (0, 1, -1)


def derivative_table():
    points = np.array(
        [
            -1.0,
            -0.8717401485096066,
            -0.5917001814331423,
            -0.2092992179024789,
            0.2092992179024789,
            0.5917001814331423,
            0.8717401485096066,
            1.0,
        ]
    )
    previous = np.ones(8)
    current = points * 1.0
    for order in range(1, 7):
        following = ((2 * order + 1) * points * current - order * previous) / (order + 1)
        previous = current
        current = following
    spacing = points[:, None] - points[None, :] + np.eye(8)
    off_diagonal = current[:, None] / (current[None, :] * spacing)
    positions = np.arange(8)
    end_values = np.where(positions == 0, -14.0, 0.0) + np.where(positions == 7, 14.0, 0.0)
    return np.where(np.eye(8) > 0, np.eye(8) * end_values[None, :], off_diagonal)


def message_rows(sent):
    own = tuple(range(1, 9))
    for place, (dx, dy) in enumerate(DIRECTIONS):
        xs = sent[dx] if dx else own
        ys = sent[dy] if dy else own
        if dy:
            pairs = [(x, y) for y in ys for x in xs]
        else:
            pairs = [(x, y) for x in xs for y in ys]
        for number, (x, y) in enumerate(pairs):
            yield STARTS[place] + number, x, y


def node_row(x, y):
    return (x - 1) * 8 + y - 1


def slot_row(x, y):
    return x * 16 + y


def selections():
    gather_to = {1: (0, 1), -1: (8, 9)}
    scatter_to = {1: (1, 2), -1: (7, 8)}
    unpack_gather = np.zeros((160, 160))
    unpack_scatter = np.zeros((64, 256))
    for x in range(1, 9):
        for y in range(1, 9):
            unpack_gather[slot_row(x, y), node_row(x, y)] = 1
            unpack_scatter[node_row(x, y), slot_row(x, y)] = 1
    for row, x, y in message_rows(gather_to):
        unpack_gather[slot_row(x, y), 64 + row] = 1
    for row, x, y in message_rows(scatter_to):
        unpack_scatter[node_row(x, y), 160 + row] = 1
    derivative = derivative_table()
    eye = np.eye(8)
    plane = np.concatenate([np.kron(derivative, eye), np.kron(eye, derivative)], 0)
    high = np.asarray(np.asarray(plane, BF16), np.float64)
    low = plane - high
    table = np.zeros((416, 256))
    for start, part in (
        (0, unpack_gather),
        (160, unpack_scatter),
        (224, np.concatenate([high, high, low], 1)),
        (352, np.concatenate([high.T, low.T], 1)),
    ):
        table[start : start + part.shape[0], : part.shape[1]] = part
    return table


def message(faces, columns):
    rows = list(faces)
    for pair in columns:
        rows += [nodes for _, nodes, _ in pair]
    blank = jnp.zeros((4,) + rows[0].shape[1:], F32)
    for side in (2, 0):
        for pair in columns:
            rows += [layer[side] for layer in pair] + [blank]
    return jnp.concatenate(rows, 0)


def gather_message(field):
    cube = field.reshape(8, 8, field.shape[1])
    columns = []
    for pair in ((6, 7), (0, 1)):
        layers = [cube[:, y, :] for y in pair]
        columns.append([(layer[0:2], layer, layer[6:8]) for layer in layers])
    return message((field[48:64], field[0:16]), columns)


def scatter_message(extended):
    cube = extended.reshape(10, 16, extended.shape[1])
    columns = []
    for pair in ((8, 9), (0, 1)):
        layers = [cube[:, y, :] for y in pair]
        columns.append([(layer[0:2], layer[1:9], layer[8:10]) for layer in layers])
    return message([cube[x, 1:9] for x in (8, 9, 0, 1)], columns)


def halves(value):
    high = value.astype(BF16)
    return high, (value - high.astype(F32)).astype(BF16)


def product(left, right, dims=((1,), (0,))):
    return lax.dot_general(left, right, (dims, ((), ())), preferred_element_type=F32)


def pick(chooser, value):
    high, low = halves(value)
    return product(chooser, low) + product(chooser, high)


def times(value, high_ref, low_ref, dims=((1,), (0,))):
    high, low = halves(value)
    return (
        product(low, high_ref[...], dims)
        + product(high, low_ref[...], dims)
        + product(high, high_ref[...], dims)
    )


def place(value, chooser, dims):
    total = None
    for piece in pieces(value):
        part = lax.dot_general(piece, chooser, (dims, ((), ())), preferred_element_type=F32)
        total = part if total is None else total + part
    return total


def kernel(
    counts,
    right_hbm,
    geometry_hbm,
    element_hbm,
    vectors_hbm,
    values_hbm,
    select_hbm,
    deep_hbm,
    result_ref,
    right_ref,
    geometry_ref,
    element_ref,
    vectors_ref,
    values_ref,
    select_ref,
    deep_ref,
    start_send,
    start_recv,
    right_recv,
    geometry_recv,
    class_recv,
    wide_geometry,
    class_ref,
    entries_ref,
    own_ref,
    beside_ref,
    deep_high,
    deep_low,
    plane_send,
    plane_recv,
    first_ref,
    second_ref,
    second_back_ref,
    third_high,
    third_low,
    back_high,
    back_low,
    inverse_ref,
    sums_plane,
    sums_line,
    load_sems,
    start_sems,
    deep_sems,
    plane_sems,
    sum_send_sems,
    sum_plane_sems,
    line_send_sems,
    sum_line_sems,
):
    nx, ny, nz = counts
    gx, gy, gz = lax.axis_index("gx"), lax.axis_index("gy"), lax.axis_index("gz")
    plane_size = nx * ny
    me_plane = gx * ny + gy

    loads = [
        pltpu.make_async_copy(source, target, load_sems.at[number])
        for number, (source, target) in enumerate(
            (
                (right_hbm, right_ref),
                (select_hbm, select_ref),
                (element_hbm, element_ref),
                (vectors_hbm, vectors_ref),
                (values_hbm, values_ref),
                (deep_hbm, deep_ref),
                (geometry_hbm, geometry_ref),
            )
        )
    ]
    for load in loads:
        load.start()

    start_recv[...] = jnp.zeros_like(start_recv)
    right_recv[...] = jnp.zeros_like(right_recv)
    geometry_recv[...] = jnp.zeros_like(geometry_recv)
    class_recv[...] = jnp.zeros_like(class_recv)
    plane_recv[...] = jnp.zeros_like(plane_recv)

    def plane_partner(offset):
        other = lax.rem(me_plane + offset, plane_size)
        return other, (other // ny, lax.rem(other, ny), gz)

    def line_partner(offset):
        other = lax.rem(gz + offset, nz)
        return other, (gx, gy, other)

    class_ref[...] = jnp.zeros_like(class_ref)

    def exists(dx, dy, dz):
        x, y, z = gx + dx, gy + dy, gz + dz
        return (x >= 0) & (x < nx) & (y >= 0) & (y < ny) & (z >= 0) & (z < nz)

    barrier = pltpu.get_barrier_semaphore()
    for offset in range(1, plane_size):
        pl.semaphore_signal(
            barrier, inc=1, device_id=plane_partner(offset)[1], device_id_type=MESH
        )
    for offset in range(1, nz):
        pl.semaphore_signal(barrier, inc=1, device_id=line_partner(offset)[1], device_id_type=MESH)
    slanted = [(dx, dy, dz) for dz in (1, -1) for dx, dy in DIRECTIONS]
    partners = plane_size + nz - 2
    for step in slanted:
        pl.when(exists(*step))(
            lambda step=step: pl.semaphore_signal(
                barrier,
                inc=1,
                device_id=(gx + step[0], gy + step[1], gz + step[2]),
                device_id_type=MESH,
            )
        )
        partners = partners + exists(*step).astype(jnp.int32)
    pl.semaphore_wait(barrier, partners)

    inputs = (
        (right_hbm, right_recv),
        (class_ref, class_recv),
        (geometry_hbm, geometry_recv),
    )

    def deep_copy(number, step):
        side = 0 if step > 0 else 1
        mine, theirs = inputs[number]
        return pltpu.make_async_remote_copy(
            src_ref=mine,
            dst_ref=theirs.at[side],
            send_sem=deep_sems.at[0, number, side],
            recv_sem=deep_sems.at[1, number, side],
            device_id=(gx, gy, gz + step),
            device_id_type=MESH,
        )

    def deep_exists(step):
        return gz + 1 < nz if step > 0 else gz > 0

    def deep_start(number):
        for step in (1, -1):
            pl.when(deep_exists(step))(lambda step=step: deep_copy(number, step).start())

    def deep_wait(number):
        for step in (1, -1):
            pl.when(deep_exists(-step))(lambda step=step: deep_copy(number, step).wait_recv())

    def widen(own, received):
        half = lax.broadcasted_iota(jnp.int32, own.shape, 1) < 64
        return jnp.concatenate([own, jnp.where(half, received[1], received[0])], 1)

    def plane_copy(number, at):
        dx, dy = DIRECTIONS[at]
        rows = pl.ds(STARTS[at], STARTS[at + 1] - STARTS[at])
        return pltpu.make_async_remote_copy(
            src_ref=plane_send.at[number, rows],
            dst_ref=plane_recv.at[number, rows],
            send_sem=plane_sems.at[0, number, at],
            recv_sem=plane_sems.at[1, number, at],
            device_id=(gx + dx, gy + dy, gz),
            device_id_type=MESH,
        )

    def plane_exists(dx, dy):
        return exists(dx, dy, 0)

    def start_copy(level, at):
        dx, dy = DIRECTIONS[at]
        rows = pl.ds(STARTS[at], STARTS[at + 1] - STARTS[at])
        return pltpu.make_async_remote_copy(
            src_ref=start_send.at[rows],
            dst_ref=start_recv.at[level, rows],
            send_sem=start_sems.at[0, level, at],
            recv_sem=start_sems.at[1, level, at],
            device_id=(gx + dx, gy + dy, gz + LEVELS[level]),
            device_id_type=MESH,
        )

    def start_each(action, sign):
        for level, dz in enumerate(LEVELS):
            for at, (dx, dy) in enumerate(DIRECTIONS):
                pl.when(exists(sign * dx, sign * dy, sign * dz))(
                    lambda level=level, at=at: action(start_copy(level, at))
                )

    def plane_start(number, message):
        plane_send[number] = message
        for at, (dx, dy) in enumerate(DIRECTIONS):
            pl.when(plane_exists(dx, dy))(lambda at=at: plane_copy(number, at).start())

    def plane_wait(number):
        for at, (dx, dy) in enumerate(DIRECTIONS):
            pl.when(plane_exists(-dx, -dy))(lambda at=at: plane_copy(number, at).wait_recv())
        return plane_recv[number]

    rows = lax.broadcasted_iota(jnp.int32, (64, 128), 0)
    lanes = lax.broadcasted_iota(jnp.int32, (64, 128), 1)
    plain = ((1,), (0,))
    rows_rows = ((1,), (1,))

    def sum_deep(field):
        node = lax.rem(lax.broadcasted_iota(jnp.int32, (64, 256), 1), 8)
        following = jnp.where(node == 7, pltpu.roll(field, 255, 1), 0.0)
        previous = jnp.where(node == 0, pltpu.roll(field, 1, 1), 0.0)
        return field + following + previous

    def gather_plane_start(number, wide):
        plane_start(number, gather_message(wide))

    def gather_plane_end(wide, received):
        both = jnp.concatenate([wide, received], 0)
        return pick(select_ref[0:160, 0:160], both)

    def scatter(number, extended):
        plane_start(number, scatter_message(extended))
        both = jnp.concatenate([extended, plane_wait(number)], 0)
        return pick(select_ref[160:224, :], both)

    def solve(extended):
        value = times(extended, third_high, third_low).reshape(10, 16, 256)
        value = value.reshape(10, 1, 2, 8, 256)
        total = first_ref[0][:, None] * value[0]
        for a in range(1, 10):
            total = total + first_ref[a][:, None] * value[a]
        value = total.reshape(10, 16, 256)
        total = second_ref[0][None] * value[:, 0:1, :]
        for b in range(1, 10):
            total = total + second_ref[b][None] * value[:, b : b + 1, :]
        value = total * inverse_ref[...]
        total = second_back_ref[0][None] * value[:, 0:1, :]
        for n in range(1, 10):
            total = total + second_back_ref[n][None] * value[:, n : n + 1, :]
        value = total.reshape(10, 1, 2, 8, 256)
        total = first_ref[:, 0][:, None] * value[0]
        for m in range(1, 10):
            total = total + first_ref[:, m][:, None] * value[m]
        return times(total.reshape(160, 256), back_high, back_low, rows_rows)

    def slopes_of(field):
        high, low = halves(field)
        slopes = product(select_ref[224:352, 0:192], jnp.concatenate([high, low, high], 0))
        return slopes, times(field, deep_high, deep_low)

    def local(field, slopes, deep):
        high, low = halves(wide_geometry[0:128] * slopes)
        back = (
            product(select_ref[352:416, 0:128], low)
            + product(select_ref[352:416, 128:256], high)
            + product(select_ref[352:416, 0:128], high)
        )
        deep = times(wide_geometry[128:192] * deep, deep_high, deep_low, rows_rows)
        return back + deep + wide_geometry[192:256] * field

    def factor(inside, length, device, devices):
        last = (device == devices - 1) & (inside == length - 1)
        first = (device == 0) & (inside == 0)
        node = lax.rem(inside, 8)
        shared = ((node == 7) & ~last) | ((node == 0) & ~first)
        return jnp.where(shared, 0.5, 1.0).astype(F32)

    plane_weight = factor(rows // 8, 8, gx, nx) * factor(lax.rem(rows, 8), 8, gy, ny)
    weight = plane_weight * factor(lanes, 128, gz, nz)
    deep_start(0)
    loads[0].wait()
    right = right_ref[...]
    weighted = weight * right
    start_send[...] = gather_message(plane_weight * right)
    start_each(lambda copy: copy.start(), 1)
    loads[2].wait()
    class_ref[0:1, 0:16] = element_ref[...].astype(F32)
    deep_start(1)
    deep_start(2)
    for load in loads[1:2] + loads[3:]:
        load.wait()

    blank = jnp.zeros((6, 32), F32)
    groups = (
        [vectors_ref[a, :, 0, :] for a in range(10)]
        + [vectors_ref[b, :, 1, :] for b in range(10)]
        + [vectors_ref[:, n, 1, :] for n in range(10)]
        + [vectors_ref[:, p, 2, :] for p in range(10)]
        + [values_ref[:, d, :] for d in (1, 0, 2)]
    )
    entries = jnp.concatenate([part for group in groups for part in (group, blank)], 0)
    entries_ref[...] = jnp.concatenate(halves(entries), 1)
    corner = lax.broadcasted_iota(jnp.int32, (256, 256), 0) // 8
    along = lax.broadcasted_iota(jnp.int32, (256, 256), 1) // 8
    high, low = halves(jnp.where(corner == along, jnp.concatenate([deep_ref[...]] * 32, 0), 0.0))
    deep_high[...] = high
    deep_low[...] = low
    def element_of(shape):
        place_at = lax.rem(lax.broadcasted_iota(jnp.int32, shape, 1), 24)
        return jnp.where(place_at < 20, place_at, place_at - 24)

    node = lax.broadcasted_iota(jnp.int32, (256, 256), 0)
    node = jnp.where(node < 192, node, node - 256)
    element = element_of((256, 256))
    reach = node - 8 * element
    inside = (
        (16 * gz + element >= 0)
        & (16 * gz + element < 16 * nz)
        & (128 * gz + node >= 0)
        & (128 * gz + node < 128 * nz)
    )
    beside = (reach == -2) | (reach == -1) | (reach == 8) | (reach == 9)
    own_ref[...] = jnp.where(inside & (reach >= 0) & (reach < 8), 1.0, 0.0)
    beside_ref[...] = jnp.where(inside & beside, 1.0, 0.0)
    deep_wait(1)

    source = lax.broadcasted_iota(jnp.int32, (384, 256), 0)
    source = jnp.where(source < 128, source, jnp.where(source < 256, source - 112, source - 272))
    known = jnp.concatenate([class_ref[...], class_recv[1], class_recv[0]], 1).astype(BF16)
    classes = jnp.dot(
        known,
        (source == element_of((384, 256))).astype(F32).astype(BF16),
        preferred_element_type=F32,
    )[0:1]
    kind = lax.rem(lax.broadcasted_iota(jnp.int32, (64, 256), 0), 32).astype(F32)
    chooser = (jnp.abs(kind - classes) < 0.5).astype(F32).astype(BF16)
    table = product(entries_ref[...], chooser)
    for a in range(10):
        for m in range(10):
            first_ref[a, m] = jnp.broadcast_to(table[a * 16 + m : a * 16 + m + 1], (8, 256))
    second_ref[...] = table[160:320].reshape(10, 16, 256)
    second_back_ref[...] = table[320:480].reshape(10, 16, 256)
    mode = lax.broadcasted_iota(jnp.int32, (1, 256), 1) // 24
    third = jnp.zeros((16, 256), F32)
    level = jnp.zeros((1, 256), F32)
    for p in range(10):
        third = third + jnp.where(mode == p, table[480 + 16 * p : 496 + 16 * p], 0.0)
        level = level + jnp.where(mode == p, table[672 + p : 673 + p], 0.0)

    for m in range(10):
        inverse_ref[m] = 1.0 / (table[656 + m : 657 + m] + table[640:656] + level)
    ends = [third[c : c + 1] for c in (8, 9, 0, 1)]
    none = jnp.zeros((4, 256), F32)
    inner = third[1:9]
    reached = jnp.concatenate([none[0:1], ends[1], none, ends[2], none[0:1]], 0)
    shared = jnp.concatenate([ends[0], ends[1], none, ends[2], ends[3]], 0)
    for outer, high_ref, low_ref in (
        (reached, third_high, third_low),
        (shared, back_high, back_low),
    ):
        for group in range(16):
            at = pl.ds(16 * group, 16)
            spread = own_ref[at] * jnp.concatenate([inner] * 2, 0) + beside_ref[
                at
            ] * jnp.concatenate([outer] * 2, 0)
            high_ref[at], low_ref[at] = halves(spread)

    deep_wait(0)
    start_each(lambda copy: copy.wait_recv(), -1)
    wide = jnp.concatenate([plane_weight, plane_weight], 1) * widen(right, right_recv[...])
    extended = gather_plane_end(
        wide, widen(start_recv[0], (start_recv[1], start_recv[2]))
    )
    wide_precond = scatter(1, solve(extended))
    deep_wait(2)
    wide_geometry[...] = widen(geometry_ref[...], geometry_recv[...])
    image_local = local(wide_precond, *slopes_of(wide_precond))
    wide = sum_deep(image_local)
    gather_plane_start(2, wide)
    extended = gather_plane_end(wide, plane_wait(2))
    image = jnp.concatenate(
        [extended[16 * x + 1 : 16 * x + 9, 0:128] for x in range(1, 9)], 0
    )
    wide_again = scatter(3, solve(extended))
    slopes, deep = slopes_of(wide_again)
    precond, again = wide_precond[:, 0:128], wide_again[:, 0:128]

    own = geometry_ref[...]
    energy = (
        own[0:64] * slopes[0:64, 0:128] * slopes[0:64, 0:128]
        + own[64:128] * slopes[64:128, 0:128] * slopes[64:128, 0:128]
        + own[128:192] * deep[:, 0:128] * deep[:, 0:128]
        + own[192:256] * again * again
    )
    products = (
        weighted * precond,
        precond * image_local[:, 0:128],
        weighted * again,
        weight * image * again,
        energy,
    )
    kind = lax.broadcasted_iota(jnp.int32, (8, 128), 0)
    packed = jnp.zeros((8, 128), F32)
    for number, entry in enumerate(products):
        packed = packed + jnp.where(kind == number, jnp.sum(entry, 0, keepdims=True), 0.0)

    def sum_copy(buffer, send_sems, recv_sems, offset, mine, partner):
        return pltpu.make_async_remote_copy(
            src_ref=buffer.at[mine],
            dst_ref=buffer.at[mine],
            send_sem=send_sems.at[offset - 1],
            recv_sem=recv_sems.at[mine],
            device_id=partner,
            device_id_type=MESH,
        )

    def sum_wait(buffer, recv_sems, other):
        pltpu.make_async_copy(buffer.at[other], buffer.at[other], recv_sems.at[other]).wait()

    sums_plane[me_plane] = packed
    for offset in range(1, plane_size):
        sum_copy(
            sums_plane, sum_send_sems, sum_plane_sems, offset, me_plane, plane_partner(offset)[1]
        ).start()
    wide = sum_deep(local(wide_again, slopes, deep))
    gather_plane_start(4, wide)
    for offset in range(1, plane_size):
        sum_wait(sums_plane, sum_plane_sems, plane_partner(offset)[0])
    sums_line[gz] = jnp.sum(sums_plane[...], 0)
    for offset in range(1, nz):
        sum_copy(
            sums_line, line_send_sems, sum_line_sems, offset, gz, line_partner(offset)[1]
        ).start()
    extended = gather_plane_end(wide, plane_wait(4))
    again_image = jnp.concatenate(
        [extended[16 * x + 1 : 16 * x + 9, 0:128] for x in range(1, 9)], 0
    )
    for number in range(3):
        for step in (1, -1):
            pl.when(deep_exists(step))(
                lambda number=number, step=step: deep_copy(number, step).wait_send()
            )
    start_each(lambda copy: copy.wait_send(), 1)
    for number in range(1, ROUNDS):
        for at, (dx, dy) in enumerate(DIRECTIONS):
            pl.when(plane_exists(dx, dy))(
                lambda number=number, at=at: plane_copy(number, at).wait_send()
            )
    for offset in range(1, plane_size):
        sum_copy(
            sums_plane, sum_send_sems, sum_plane_sems, offset, me_plane, plane_partner(offset)[1]
        ).wait_send()
    for offset in range(1, nz):
        sum_copy(
            sums_line, line_send_sems, sum_line_sems, offset, gz, line_partner(offset)[1]
        ).wait_send()

    for offset in range(1, nz):
        sum_wait(sums_line, sum_line_sems, line_partner(offset)[0])
    sums = jnp.sum(jnp.sum(sums_line[...], 0), 1, keepdims=True)
    a, b, c, d, f = [sums[k : k + 1] for k in range(5)]
    step_one = a / b
    rho = a - step_one * (b + c) + step_one * step_one * d
    stretch = 1.0 + rho / a
    curvature = stretch * stretch * b - 2.0 * stretch * step_one * d + step_one * step_one * f
    step_two = rho / curvature
    on_precond = step_one + step_two * stretch
    on_again = step_one * step_two
    result_ref[0] = on_precond * precond - on_again * again
    result_ref[1] = right - on_precond * image + on_again * again_image


def on_device(counts, right_side, geometry, element_shape_class, fdm_vectors, fdm_values):
    nx, ny, nz = counts
    shape = right_side.shape
    vmem = pl.BlockSpec(memory_space=pltpu.VMEM)
    result = pl.pallas_call(
        lambda *refs: kernel(counts, *refs),
        out_shape=jax.ShapeDtypeStruct((2, 64, 128), F32),
        in_specs=[pl.BlockSpec(memory_space=pl.ANY)] * 7,
        out_specs=vmem,
        scratch_shapes=[
            pltpu.VMEM((64, 128), F32),
            pltpu.VMEM((256, 128), F32),
            pltpu.VMEM((1, 16), jnp.int32),
            pltpu.VMEM((10, 10, 3, 32), F32),
            pltpu.VMEM((10, 3, 32), F32),
            pltpu.VMEM((416, 256), BF16),
            pltpu.VMEM((8, 256), F32),
            pltpu.VMEM((96, 128), F32),
            pltpu.VMEM((3, 96, 128), F32),
            pltpu.VMEM((2, 64, 128), F32),
            pltpu.VMEM((2, 256, 128), F32),
            pltpu.VMEM((2, 8, 128), F32),
            pltpu.VMEM((256, 256), F32),
            pltpu.VMEM((8, 128), F32),
            pltpu.VMEM((688, 64), BF16),
            pltpu.VMEM((256, 256), F32),
            pltpu.VMEM((256, 256), F32),
            pltpu.VMEM((256, 256), BF16),
            pltpu.VMEM((256, 256), BF16),
            pltpu.VMEM((ROUNDS, 96, 256), F32),
            pltpu.VMEM((ROUNDS, 96, 256), F32),
            pltpu.VMEM((10, 10, 8, 256), F32),
            pltpu.VMEM((10, 16, 256), F32),
            pltpu.VMEM((10, 16, 256), F32),
            pltpu.VMEM((256, 256), BF16),
            pltpu.VMEM((256, 256), BF16),
            pltpu.VMEM((256, 256), BF16),
            pltpu.VMEM((256, 256), BF16),
            pltpu.VMEM((10, 16, 256), F32),
            pltpu.VMEM((nx * ny, 8, 128), F32),
            pltpu.VMEM((nz, 8, 128), F32),
            pltpu.SemaphoreType.DMA((7,)),
            pltpu.SemaphoreType.DMA((2, 3, 8)),
            pltpu.SemaphoreType.DMA((2, 3, 2)),
            pltpu.SemaphoreType.DMA((2, ROUNDS, 8)),
            pltpu.SemaphoreType.DMA((nx * ny,)),
            pltpu.SemaphoreType.DMA((nx * ny,)),
            pltpu.SemaphoreType.DMA((nz,)),
            pltpu.SemaphoreType.DMA((nz,)),
        ],
        compiler_params=pltpu.CompilerParams(
            collective_id=0, has_side_effects=True, vmem_limit_bytes=60 * 1024 * 1024
        ),
    )(
        right_side.reshape(64, 128),
        geometry.reshape(256, 128),
        element_shape_class.reshape(1, 16),
        jnp.transpose(fdm_vectors, (2, 3, 1, 0)),
        jnp.transpose(fdm_values, (2, 1, 0)),
        jnp.asarray(selections(), BF16),
        jnp.asarray(np.tile(derivative_table().T, (1, 32)), F32),
    )
    return result[0].reshape(shape), result[1].reshape(shape)


def solution(mesh):
    counts = tuple(mesh.shape[name] for name in ("gx", "gy", "gz"))
    placed = (P("gx", "gy", "gz"), P(None, "gx", "gy", "gz"), P("gx", "gy", "gz"), P(), P())
    return jax.shard_map(
        lambda *arrays: on_device(counts, *arrays),
        mesh=mesh,
        in_specs=placed,
        out_specs=(P("gx", "gy", "gz"), P("gx", "gy", "gz")),
        check_vma=False,
    )
```

```python
import jax
import jax.numpy as jnp
import numpy as np
from jax import lax
from jax.experimental import pallas as pl
from jax.experimental.pallas import tpu as pltpu
from jax.sharding import PartitionSpec as P

MESH = pl.DeviceIdType.MESH
F32 = jnp.float32
BF16 = jnp.bfloat16
DIRECTIONS = ((1, 0), (-1, 0), (0, 1), (0, -1), (1, 1), (1, -1), (-1, 1), (-1, -1))
STARTS = (0, 16, 32, 48, 64, 72, 80, 88, 96)
ROUNDS = 5
LEVELS = (0, 1, -1)


def derivative_table():
    points = np.array(
        [
            -1.0,
            -0.8717401485096066,
            -0.5917001814331423,
            -0.2092992179024789,
            0.2092992179024789,
            0.5917001814331423,
            0.8717401485096066,
            1.0,
        ]
    )
    previous = np.ones(8)
    current = points * 1.0
    for order in range(1, 7):
        following = ((2 * order + 1) * points * current - order * previous) / (order + 1)
        previous = current
        current = following
    spacing = points[:, None] - points[None, :] + np.eye(8)
    off_diagonal = current[:, None] / (current[None, :] * spacing)
    positions = np.arange(8)
    end_values = np.where(positions == 0, -14.0, 0.0) + np.where(positions == 7, 14.0, 0.0)
    return np.where(np.eye(8) > 0, np.eye(8) * end_values[None, :], off_diagonal)


def message_rows(sent):
    own = tuple(range(1, 9))
    for place, (dx, dy) in enumerate(DIRECTIONS):
        xs = sent[dx] if dx else own
        ys = sent[dy] if dy else own
        if dy:
            pairs = [(x, y) for y in ys for x in xs]
        else:
            pairs = [(x, y) for x in xs for y in ys]
        for number, (x, y) in enumerate(pairs):
            yield STARTS[place] + number, x, y


def node_row(x, y):
    return (x - 1) * 8 + y - 1


def slot_row(x, y):
    return x * 16 + y


def selections():
    gather_to = {1: (0, 1), -1: (8, 9)}
    scatter_to = {1: (1, 2), -1: (7, 8)}
    unpack_gather = np.zeros((160, 160))
    unpack_scatter = np.zeros((64, 256))
    for x in range(1, 9):
        for y in range(1, 9):
            unpack_gather[slot_row(x, y), node_row(x, y)] = 1
            unpack_scatter[node_row(x, y), slot_row(x, y)] = 1
    for row, x, y in message_rows(gather_to):
        unpack_gather[slot_row(x, y), 64 + row] = 1
    for row, x, y in message_rows(scatter_to):
        unpack_scatter[node_row(x, y), 160 + row] = 1
    derivative = derivative_table()
    eye = np.eye(8)
    plane = np.concatenate([np.kron(derivative, eye), np.kron(eye, derivative)], 0)
    high = np.asarray(np.asarray(plane, BF16), np.float64)
    low = plane - high
    table = np.zeros((416, 256))
    for start, part in (
        (0, unpack_gather),
        (160, unpack_scatter),
        (224, np.concatenate([high, high, low], 1)),
        (352, np.concatenate([high.T, low.T], 1)),
    ):
        table[start : start + part.shape[0], : part.shape[1]] = part
    return table


def message(faces, columns):
    rows = list(faces)
    for pair in columns:
        rows += [nodes for _, nodes, _ in pair]
    blank = jnp.zeros((4,) + rows[0].shape[1:], F32)
    for side in (2, 0):
        for pair in columns:
            rows += [layer[side] for layer in pair] + [blank]
    return jnp.concatenate(rows, 0)


def gather_message(field):
    cube = field.reshape(8, 8, field.shape[1])
    columns = []
    for pair in ((6, 7), (0, 1)):
        layers = [cube[:, y, :] for y in pair]
        columns.append([(layer[0:2], layer, layer[6:8]) for layer in layers])
    return message((field[48:64], field[0:16]), columns)


def scatter_message(extended):
    cube = extended.reshape(10, 16, extended.shape[1])
    columns = []
    for pair in ((8, 9), (0, 1)):
        layers = [cube[:, y, :] for y in pair]
        columns.append([(layer[0:2], layer[1:9], layer[8:10]) for layer in layers])
    return message([cube[x, 1:9] for x in (8, 9, 0, 1)], columns)


def halves(value):
    high = value.astype(BF16)
    return high, (value - high.astype(F32)).astype(BF16)


def product(left, right, dims=((1,), (0,))):
    return lax.dot_general(left, right, (dims, ((), ())), preferred_element_type=F32)


def pick(chooser, value):
    high, low = halves(value)
    return product(chooser, low) + product(chooser, high)


def times(value, high_ref, low_ref, dims=((1,), (0,))):
    high, low = halves(value)
    return (
        product(low, high_ref[...], dims)
        + product(high, low_ref[...], dims)
        + product(high, high_ref[...], dims)
    )


def place(value, chooser, dims):
    total = None
    for piece in pieces(value):
        part = lax.dot_general(piece, chooser, (dims, ((), ())), preferred_element_type=F32)
        total = part if total is None else total + part
    return total


def kernel(
    counts,
    right_hbm,
    geometry_hbm,
    element_hbm,
    vectors_hbm,
    values_hbm,
    select_hbm,
    deep_hbm,
    result_ref,
    right_ref,
    geometry_ref,
    element_ref,
    vectors_ref,
    values_ref,
    select_ref,
    deep_ref,
    start_send,
    start_recv,
    right_recv,
    geometry_recv,
    class_recv,
    wide_geometry,
    image_ref,
    class_ref,
    entries_ref,
    own_ref,
    beside_ref,
    deep_high,
    deep_low,
    plane_send,
    plane_recv,
    first_ref,
    second_ref,
    second_back_ref,
    third_high,
    third_low,
    back_high,
    back_low,
    inverse_ref,
    sums_plane,
    sums_line,
    load_sems,
    start_sems,
    deep_sems,
    plane_sems,
    sum_send_sems,
    sum_plane_sems,
    line_send_sems,
    sum_line_sems,
):
    nx, ny, nz = counts
    gx, gy, gz = lax.axis_index("gx"), lax.axis_index("gy"), lax.axis_index("gz")
    plane_size = nx * ny
    me_plane = gx * ny + gy

    loads = [
        pltpu.make_async_copy(source, target, load_sems.at[number])
        for number, (source, target) in enumerate(
            (
                (right_hbm, right_ref),
                (select_hbm, select_ref),
                (element_hbm, element_ref),
                (vectors_hbm, vectors_ref),
                (values_hbm, values_ref),
                (deep_hbm, deep_ref),
                (geometry_hbm, geometry_ref),
            )
        )
    ]
    for load in loads:
        load.start()

    start_recv[...] = jnp.zeros_like(start_recv)
    right_recv[...] = jnp.zeros_like(right_recv)
    geometry_recv[...] = jnp.zeros_like(geometry_recv)
    class_recv[...] = jnp.zeros_like(class_recv)
    plane_recv[...] = jnp.zeros_like(plane_recv)

    def plane_partner(offset):
        other = lax.rem(me_plane + offset, plane_size)
        return other, (other // ny, lax.rem(other, ny), gz)

    def line_partner(offset):
        other = lax.rem(gz + offset, nz)
        return other, (gx, gy, other)

    class_ref[...] = jnp.zeros_like(class_ref)

    def exists(dx, dy, dz):
        x, y, z = gx + dx, gy + dy, gz + dz
        return (x >= 0) & (x < nx) & (y >= 0) & (y < ny) & (z >= 0) & (z < nz)

    barrier = pltpu.get_barrier_semaphore()
    for offset in range(1, plane_size):
        pl.semaphore_signal(
            barrier, inc=1, device_id=plane_partner(offset)[1], device_id_type=MESH
        )
    for offset in range(1, nz):
        pl.semaphore_signal(barrier, inc=1, device_id=line_partner(offset)[1], device_id_type=MESH)
    slanted = [(dx, dy, dz) for dz in (1, -1) for dx, dy in DIRECTIONS]
    partners = plane_size + nz - 2
    for step in slanted:
        pl.when(exists(*step))(
            lambda step=step: pl.semaphore_signal(
                barrier,
                inc=1,
                device_id=(gx + step[0], gy + step[1], gz + step[2]),
                device_id_type=MESH,
            )
        )
        partners = partners + exists(*step).astype(jnp.int32)
    pl.semaphore_wait(barrier, partners)

    inputs = (
        (right_hbm, right_recv),
        (class_ref, class_recv),
        (geometry_hbm, geometry_recv),
    )

    def deep_copy(number, step):
        side = 0 if step > 0 else 1
        mine, theirs = inputs[number]
        return pltpu.make_async_remote_copy(
            src_ref=mine,
            dst_ref=theirs.at[side],
            send_sem=deep_sems.at[0, number, side],
            recv_sem=deep_sems.at[1, number, side],
            device_id=(gx, gy, gz + step),
            device_id_type=MESH,
        )

    def deep_exists(step):
        return gz + 1 < nz if step > 0 else gz > 0

    def deep_start(number):
        for step in (1, -1):
            pl.when(deep_exists(step))(lambda step=step: deep_copy(number, step).start())

    def deep_wait(number):
        for step in (1, -1):
            pl.when(deep_exists(-step))(lambda step=step: deep_copy(number, step).wait_recv())

    def widen(own, received):
        half = lax.broadcasted_iota(jnp.int32, own.shape, 1) < 64
        return jnp.concatenate([own, jnp.where(half, received[1], received[0])], 1)

    def plane_copy(number, at):
        dx, dy = DIRECTIONS[at]
        rows = pl.ds(STARTS[at], STARTS[at + 1] - STARTS[at])
        return pltpu.make_async_remote_copy(
            src_ref=plane_send.at[number, rows],
            dst_ref=plane_recv.at[number, rows],
            send_sem=plane_sems.at[0, number, at],
            recv_sem=plane_sems.at[1, number, at],
            device_id=(gx + dx, gy + dy, gz),
            device_id_type=MESH,
        )

    def plane_exists(dx, dy):
        return exists(dx, dy, 0)

    def start_copy(level, at):
        dx, dy = DIRECTIONS[at]
        rows = pl.ds(STARTS[at], STARTS[at + 1] - STARTS[at])
        return pltpu.make_async_remote_copy(
            src_ref=start_send.at[rows],
            dst_ref=start_recv.at[level, rows],
            send_sem=start_sems.at[0, level, at],
            recv_sem=start_sems.at[1, level, at],
            device_id=(gx + dx, gy + dy, gz + LEVELS[level]),
            device_id_type=MESH,
        )

    def start_each(action, sign):
        for level, dz in enumerate(LEVELS):
            for at, (dx, dy) in enumerate(DIRECTIONS):
                pl.when(exists(sign * dx, sign * dy, sign * dz))(
                    lambda level=level, at=at: action(start_copy(level, at))
                )

    def plane_start(number, message):
        plane_send[number] = message
        for at, (dx, dy) in enumerate(DIRECTIONS):
            pl.when(plane_exists(dx, dy))(lambda at=at: plane_copy(number, at).start())

    def plane_wait(number):
        for at, (dx, dy) in enumerate(DIRECTIONS):
            pl.when(plane_exists(-dx, -dy))(lambda at=at: plane_copy(number, at).wait_recv())
        return plane_recv[number]

    rows = lax.broadcasted_iota(jnp.int32, (64, 128), 0)
    lanes = lax.broadcasted_iota(jnp.int32, (64, 128), 1)
    plain = ((1,), (0,))
    rows_rows = ((1,), (1,))

    def sum_deep(field):
        node = lax.rem(lax.broadcasted_iota(jnp.int32, (64, 256), 1), 8)
        following = jnp.where(node == 7, pltpu.roll(field, 255, 1), 0.0)
        previous = jnp.where(node == 0, pltpu.roll(field, 1, 1), 0.0)
        return field + following + previous

    def gather_plane_start(number, wide):
        plane_start(number, gather_message(wide))

    def gather_plane_end(wide, received):
        both = jnp.concatenate([wide, received], 0)
        return pick(select_ref[0:160, 0:160], both)

    def scatter(number, extended, meanwhile):
        plane_start(number, scatter_message(extended))
        meanwhile()
        both = jnp.concatenate([extended, plane_wait(number)], 0)
        return pick(select_ref[160:224, :], both)

    def solve(extended):
        value = times(extended, third_high, third_low).reshape(10, 16, 256)
        value = value.reshape(10, 1, 2, 8, 256)
        total = first_ref[0][:, None] * value[0]
        for a in range(1, 10):
            total = total + first_ref[a][:, None] * value[a]
        value = total.reshape(10, 16, 256)
        total = second_ref[0][None] * value[:, 0:1, :]
        for b in range(1, 10):
            total = total + second_ref[b][None] * value[:, b : b + 1, :]
        value = total * inverse_ref[...]
        total = second_back_ref[0][None] * value[:, 0:1, :]
        for n in range(1, 10):
            total = total + second_back_ref[n][None] * value[:, n : n + 1, :]
        value = total.reshape(10, 1, 2, 8, 256)
        total = first_ref[:, 0][:, None] * value[0]
        for m in range(1, 10):
            total = total + first_ref[:, m][:, None] * value[m]
        return times(total.reshape(160, 256), back_high, back_low, rows_rows)

    def slopes_of(field):
        high, low = halves(field)
        slopes = product(select_ref[224:352, 0:192], jnp.concatenate([high, low, high], 0))
        return slopes, times(field, deep_high, deep_low)

    def local(field, slopes, deep):
        high, low = halves(wide_geometry[0:128] * slopes)
        back = (
            product(select_ref[352:416, 0:128], low)
            + product(select_ref[352:416, 128:256], high)
            + product(select_ref[352:416, 0:128], high)
        )
        deep = times(wide_geometry[128:192] * deep, deep_high, deep_low, rows_rows)
        return back + deep + wide_geometry[192:256] * field

    def factor(inside, length, device, devices):
        last = (device == devices - 1) & (inside == length - 1)
        first = (device == 0) & (inside == 0)
        node = lax.rem(inside, 8)
        shared = ((node == 7) & ~last) | ((node == 0) & ~first)
        return jnp.where(shared, 0.5, 1.0).astype(F32)

    plane_weight = factor(rows // 8, 8, gx, nx) * factor(lax.rem(rows, 8), 8, gy, ny)
    weight = plane_weight * factor(lanes, 128, gz, nz)
    deep_start(0)
    loads[0].wait()
    right = right_ref[...]
    weighted = weight * right
    start_send[...] = gather_message(plane_weight * right)
    start_each(lambda copy: copy.start(), 1)
    loads[2].wait()
    class_ref[0:1, 0:16] = element_ref[...].astype(F32)
    deep_start(1)
    deep_start(2)
    for load in loads[1:2] + loads[3:]:
        load.wait()

    blank = jnp.zeros((6, 32), F32)
    groups = (
        [vectors_ref[a, :, 0, :] for a in range(10)]
        + [vectors_ref[b, :, 1, :] for b in range(10)]
        + [vectors_ref[:, n, 1, :] for n in range(10)]
        + [vectors_ref[:, p, 2, :] for p in range(10)]
        + [values_ref[:, d, :] for d in (1, 0, 2)]
    )
    entries = jnp.concatenate([part for group in groups for part in (group, blank)], 0)
    entries_ref[...] = jnp.concatenate(halves(entries), 1)
    corner = lax.broadcasted_iota(jnp.int32, (256, 256), 0) // 8
    along = lax.broadcasted_iota(jnp.int32, (256, 256), 1) // 8
    high, low = halves(jnp.where(corner == along, jnp.concatenate([deep_ref[...]] * 32, 0), 0.0))
    deep_high[...] = high
    deep_low[...] = low
    def element_of(shape):
        place_at = lax.rem(lax.broadcasted_iota(jnp.int32, shape, 1), 24)
        return jnp.where(place_at < 20, place_at, place_at - 24)

    node = lax.broadcasted_iota(jnp.int32, (256, 256), 0)
    node = jnp.where(node < 192, node, node - 256)
    element = element_of((256, 256))
    reach = node - 8 * element
    inside = (
        (16 * gz + element >= 0)
        & (16 * gz + element < 16 * nz)
        & (128 * gz + node >= 0)
        & (128 * gz + node < 128 * nz)
    )
    beside = (reach == -2) | (reach == -1) | (reach == 8) | (reach == 9)
    own_ref[...] = jnp.where(inside & (reach >= 0) & (reach < 8), 1.0, 0.0)
    beside_ref[...] = jnp.where(inside & beside, 1.0, 0.0)
    deep_wait(1)

    source = lax.broadcasted_iota(jnp.int32, (384, 256), 0)
    source = jnp.where(source < 128, source, jnp.where(source < 256, source - 112, source - 272))
    known = jnp.concatenate([class_ref[...], class_recv[1], class_recv[0]], 1).astype(BF16)
    classes = jnp.dot(
        known,
        (source == element_of((384, 256))).astype(F32).astype(BF16),
        preferred_element_type=F32,
    )[0:1]
    kind = lax.rem(lax.broadcasted_iota(jnp.int32, (64, 256), 0), 32).astype(F32)
    chooser = (jnp.abs(kind - classes) < 0.5).astype(F32).astype(BF16)
    table = product(entries_ref[...], chooser)
    for a in range(10):
        for m in range(10):
            first_ref[a, m] = jnp.broadcast_to(table[a * 16 + m : a * 16 + m + 1], (8, 256))
    second_ref[...] = table[160:320].reshape(10, 16, 256)
    second_back_ref[...] = table[320:480].reshape(10, 16, 256)
    mode = lax.broadcasted_iota(jnp.int32, (1, 256), 1) // 24
    third = jnp.zeros((16, 256), F32)
    level = jnp.zeros((1, 256), F32)
    for p in range(10):
        third = third + jnp.where(mode == p, table[480 + 16 * p : 496 + 16 * p], 0.0)
        level = level + jnp.where(mode == p, table[672 + p : 673 + p], 0.0)

    for m in range(10):
        inverse_ref[m] = 1.0 / (table[656 + m : 657 + m] + table[640:656] + level)
    ends = [third[c : c + 1] for c in (8, 9, 0, 1)]
    none = jnp.zeros((4, 256), F32)
    inner = third[1:9]
    reached = jnp.concatenate([none[0:1], ends[1], none, ends[2], none[0:1]], 0)
    shared = jnp.concatenate([ends[0], ends[1], none, ends[2], ends[3]], 0)
    for outer, high_ref, low_ref in (
        (reached, third_high, third_low),
        (shared, back_high, back_low),
    ):
        for group in range(16):
            at = pl.ds(16 * group, 16)
            spread = own_ref[at] * jnp.concatenate([inner] * 2, 0) + beside_ref[
                at
            ] * jnp.concatenate([outer] * 2, 0)
            high_ref[at], low_ref[at] = halves(spread)

    deep_wait(0)
    start_each(lambda copy: copy.wait_recv(), -1)
    wide = jnp.concatenate([plane_weight, plane_weight], 1) * widen(right, right_recv[...])
    extended = gather_plane_end(
        wide, widen(start_recv[0], (start_recv[1], start_recv[2]))
    )

    def load_geometry():
        deep_wait(2)
        wide_geometry[...] = widen(geometry_ref[...], geometry_recv[...])

    wide_precond = scatter(1, solve(extended), load_geometry)
    image_local = local(wide_precond, *slopes_of(wide_precond))
    wide = sum_deep(image_local)
    gather_plane_start(2, wide)
    extended = gather_plane_end(wide, plane_wait(2))

    def keep_image():
        image_ref[...] = jnp.concatenate(
            [extended[16 * x + 1 : 16 * x + 9, 0:128] for x in range(1, 9)], 0
        )

    wide_again = scatter(3, solve(extended), keep_image)
    image = image_ref[...]
    slopes, deep = slopes_of(wide_again)
    precond, again = wide_precond[:, 0:128], wide_again[:, 0:128]

    own = geometry_ref[...]
    energy = (
        own[0:64] * slopes[0:64, 0:128] * slopes[0:64, 0:128]
        + own[64:128] * slopes[64:128, 0:128] * slopes[64:128, 0:128]
        + own[128:192] * deep[:, 0:128] * deep[:, 0:128]
        + own[192:256] * again * again
    )
    products = (
        weighted * precond,
        precond * image_local[:, 0:128],
        weighted * again,
        weight * image * again,
        energy,
    )
    kind = lax.broadcasted_iota(jnp.int32, (8, 128), 0)
    packed = jnp.zeros((8, 128), F32)
    for number, entry in enumerate(products):
        packed = packed + jnp.where(kind == number, jnp.sum(entry, 0, keepdims=True), 0.0)

    def sum_copy(buffer, send_sems, recv_sems, offset, mine, partner):
        return pltpu.make_async_remote_copy(
            src_ref=buffer.at[mine],
            dst_ref=buffer.at[mine],
            send_sem=send_sems.at[offset - 1],
            recv_sem=recv_sems.at[mine],
            device_id=partner,
            device_id_type=MESH,
        )

    def sum_wait(buffer, recv_sems, other):
        pltpu.make_async_copy(buffer.at[other], buffer.at[other], recv_sems.at[other]).wait()

    sums_plane[me_plane] = packed
    for offset in range(1, plane_size):
        sum_copy(
            sums_plane, sum_send_sems, sum_plane_sems, offset, me_plane, plane_partner(offset)[1]
        ).start()
    wide = sum_deep(local(wide_again, slopes, deep))
    gather_plane_start(4, wide)
    for offset in range(1, plane_size):
        sum_wait(sums_plane, sum_plane_sems, plane_partner(offset)[0])
    sums_line[gz] = jnp.sum(sums_plane[...], 0)
    for offset in range(1, nz):
        sum_copy(
            sums_line, line_send_sems, sum_line_sems, offset, gz, line_partner(offset)[1]
        ).start()
    extended = gather_plane_end(wide, plane_wait(4))
    again_image = jnp.concatenate(
        [extended[16 * x + 1 : 16 * x + 9, 0:128] for x in range(1, 9)], 0
    )
    for number in range(3):
        for step in (1, -1):
            pl.when(deep_exists(step))(
                lambda number=number, step=step: deep_copy(number, step).wait_send()
            )
    start_each(lambda copy: copy.wait_send(), 1)
    for number in range(1, ROUNDS):
        for at, (dx, dy) in enumerate(DIRECTIONS):
            pl.when(plane_exists(dx, dy))(
                lambda number=number, at=at: plane_copy(number, at).wait_send()
            )
    for offset in range(1, plane_size):
        sum_copy(
            sums_plane, sum_send_sems, sum_plane_sems, offset, me_plane, plane_partner(offset)[1]
        ).wait_send()
    for offset in range(1, nz):
        sum_copy(
            sums_line, line_send_sems, sum_line_sems, offset, gz, line_partner(offset)[1]
        ).wait_send()

    for offset in range(1, nz):
        sum_wait(sums_line, sum_line_sems, line_partner(offset)[0])
    sums = jnp.sum(jnp.sum(sums_line[...], 0), 1, keepdims=True)
    a, b, c, d, f = [sums[k : k + 1] for k in range(5)]
    step_one = a / b
    rho = a - step_one * (b + c) + step_one * step_one * d
    stretch = 1.0 + rho / a
    curvature = stretch * stretch * b - 2.0 * stretch * step_one * d + step_one * step_one * f
    step_two = rho / curvature
    on_precond = step_one + step_two * stretch
    on_again = step_one * step_two
    result_ref[0] = on_precond * precond - on_again * again
    result_ref[1] = right - on_precond * image + on_again * again_image


def on_device(counts, right_side, geometry, element_shape_class, fdm_vectors, fdm_values):
    nx, ny, nz = counts
    shape = right_side.shape
    vmem = pl.BlockSpec(memory_space=pltpu.VMEM)
    result = pl.pallas_call(
        lambda *refs: kernel(counts, *refs),
        out_shape=jax.ShapeDtypeStruct((2, 64, 128), F32),
        in_specs=[pl.BlockSpec(memory_space=pl.ANY)] * 7,
        out_specs=vmem,
        scratch_shapes=[
            pltpu.VMEM((64, 128), F32),
            pltpu.VMEM((256, 128), F32),
            pltpu.VMEM((1, 16), jnp.int32),
            pltpu.VMEM((10, 10, 3, 32), F32),
            pltpu.VMEM((10, 3, 32), F32),
            pltpu.VMEM((416, 256), BF16),
            pltpu.VMEM((8, 256), F32),
            pltpu.VMEM((96, 128), F32),
            pltpu.VMEM((3, 96, 128), F32),
            pltpu.VMEM((2, 64, 128), F32),
            pltpu.VMEM((2, 256, 128), F32),
            pltpu.VMEM((2, 8, 128), F32),
            pltpu.VMEM((256, 256), F32),
            pltpu.VMEM((64, 128), F32),
            pltpu.VMEM((8, 128), F32),
            pltpu.VMEM((688, 64), BF16),
            pltpu.VMEM((256, 256), F32),
            pltpu.VMEM((256, 256), F32),
            pltpu.VMEM((256, 256), BF16),
            pltpu.VMEM((256, 256), BF16),
            pltpu.VMEM((ROUNDS, 96, 256), F32),
            pltpu.VMEM((ROUNDS, 96, 256), F32),
            pltpu.VMEM((10, 10, 8, 256), F32),
            pltpu.VMEM((10, 16, 256), F32),
            pltpu.VMEM((10, 16, 256), F32),
            pltpu.VMEM((256, 256), BF16),
            pltpu.VMEM((256, 256), BF16),
            pltpu.VMEM((256, 256), BF16),
            pltpu.VMEM((256, 256), BF16),
            pltpu.VMEM((10, 16, 256), F32),
            pltpu.VMEM((nx * ny, 8, 128), F32),
            pltpu.VMEM((nz, 8, 128), F32),
            pltpu.SemaphoreType.DMA((7,)),
            pltpu.SemaphoreType.DMA((2, 3, 8)),
            pltpu.SemaphoreType.DMA((2, 3, 2)),
            pltpu.SemaphoreType.DMA((2, ROUNDS, 8)),
            pltpu.SemaphoreType.DMA((nx * ny,)),
            pltpu.SemaphoreType.DMA((nx * ny,)),
            pltpu.SemaphoreType.DMA((nz,)),
            pltpu.SemaphoreType.DMA((nz,)),
        ],
        compiler_params=pltpu.CompilerParams(
            collective_id=0, has_side_effects=True, vmem_limit_bytes=60 * 1024 * 1024
        ),
    )(
        right_side.reshape(64, 128),
        geometry.reshape(256, 128),
        element_shape_class.reshape(1, 16),
        jnp.transpose(fdm_vectors, (2, 3, 1, 0)),
        jnp.transpose(fdm_values, (2, 1, 0)),
        jnp.asarray(selections(), BF16),
        jnp.asarray(np.tile(derivative_table().T, (1, 32)), F32),
    )
    return result[0].reshape(shape), result[1].reshape(shape)


def solution(mesh):
    counts = tuple(mesh.shape[name] for name in ("gx", "gy", "gz"))
    placed = (P("gx", "gy", "gz"), P(None, "gx", "gy", "gz"), P("gx", "gy", "gz"), P(), P())
    return jax.shard_map(
        lambda *arrays: on_device(counts, *arrays),
        mesh=mesh,
        in_specs=placed,
        out_specs=(P("gx", "gy", "gz"), P("gx", "gy", "gz")),
        check_vma=False,
    )
```
